32 devices in a mesh: tile: 16 (over z, y, core), layer: 2 (over x).
Axes of the slice: x: 2, y: 2, z: 4, core: 2. Of those that a mesh axis runs over, the one named last changes fastest.
Arguments:
- warmth_level: float32 [16, 16, 512], P('layer', 'tile'), may hold values from -6 to 6
- heat_flow_ability: float32 [16, 16, 512], P('layer', 'tile'), may hold values from 0.5 to 2
- material_zone_label: int32 [16, 16, 512], P('layer', 'tile'), may hold values from 0 to 3
- reciprocal_warming_storage: float32 [4], replicated, may hold values from 0.5 to 2
- collector_potential_field: float32 [16, 16, 512], P('layer', 'tile'), may hold values from -4 to 4
- tab_indicator: int32 [16, 512], P('tile'), may hold values 0 or 1
- sheet_node_link_matrix: float32 [40, 16], replicated, may hold values from -1.5 to 1.5
- solution_salt_level: float32 [40, 16, 512], P(None, 'tile', 'layer'), may hold values from -6 to 6
- grain_shell_level: float32 [32, 40, 16, 512], P(None, None, 'tile', 'layer'), may hold values from -6 to 6
- solution_diffusion_matrix: float32 [40, 40], replicated, may hold values from -1 to 1.5
- grain_diffusion_matrix: float32 [32, 32], replicated, may hold values from -1 to 1.5
Outputs:
- next_warmth_level: float32 [16, 16, 512], P('layer', 'tile')
- reaction_warming_sheets: float32 [16, 16, 512], P('layer', 'tile')
- reaction_flux_sheets: float32 [16, 16, 512], P('layer', 'tile')
- next_grain_level: float32 [32, 40, 16, 512], P(None, None, 'tile', 'layer')
- next_solution_level: float32 [40, 16, 512], P(None, 'tile', 'layer')
The draws below stay inside these ranges and needn't reach their ends.
All inputs are finite; a program needn't handle non-finite values. No bound on the sum of `tab_indicator` on one device may be relied on, other than what follows from the above.
Results may differ from the reference program's by a relative error of at most 0.0002.
Values sent between devices are 32-bit elements; how exact they have to be, the bound alone decides.
No kernel may reach another device: no remote copies, remote signals or barrier semaphores. Data moves between devices by JAX's collectives and lax.ppermute only.
A program may use at most 64 MiB of HBM per device.

```python
import math
import jax
import jax.numpy as jnp
from jax import lax

E = 40
S = 32
REGIONS = 4
SWEEPS = 3
BV_ITERS = 4
SHEET_NUMBER = 16
SPAN_ALONG_X = 16
SPAN_ALONG_Y = 512


def propagator(noise, order):
    return 0.8 * jnp.eye(order, dtype=jnp.float32) + 0.4 * noise / math.sqrt(order)


def draw_solution_diffusion_matrix(key, part):
    key = jax.random.fold_in(key, 11)
    noise = jnp.clip(jax.random.normal(key, (E, E), jnp.float32), -3.0, 3.0)
    return propagator(noise, E)


def draw_grain_diffusion_matrix(key, part):
    key = jax.random.fold_in(key, 23)
    noise = jnp.clip(jax.random.normal(key, (S, S), jnp.float32), -3.0, 3.0)
    return propagator(noise, S)


def touch_ends(array, key, low, high):
    longest = array.shape.index(max(array.shape))
    spots = []
    for shift in (0, 1):
        where = [jax.random.randint(jax.random.fold_in(key, axis), (), 0, length) for axis, length in enumerate(array.shape)]
        where[longest] = (where[longest] + shift) % array.shape[longest]
        spots.append(tuple(where))
    return array.at[spots[0]].set(low).at[spots[1]].set(high)


def levels(stream_key, dims, shards, smallest, top_value):
    def one(dim, shards_of):
        draws = jax.random.uniform(jax.random.fold_in(jax.random.fold_in(stream_key, 6), dim), (shards_of,), jnp.float32, smallest / len(shards), top_value / len(shards))
        return jnp.repeat(jnp.exp(draws), dims[dim] // shards_of).reshape((-1,) + (1,) * (len(dims) - dim - 1))

    level = one(*shards[0])
    for cut in shards[1:]:
        level = level * one(*cut)
    return level


def gaussian(stream_key, shape, scale, limit, shards=(), kind=jnp.bfloat16):
    result = jax.random.normal(stream_key, shape, jnp.float32) * scale
    if len(shards) > 0:
        result = levels(stream_key, shape, shards, -0.22, 0.18) * result
    return jnp.clip(result, min=-limit, max=limit).astype(kind)


def setup_inputs(seed: int = 0) -> dict:
    splits = jax.random.split(jax.random.key(seed), 12)
    return {
        "warmth_level": gaussian(splits[0], (SHEET_NUMBER, SPAN_ALONG_X, SPAN_ALONG_Y), 1.0, 6.0, ((0, 2), (1, 16)), jnp.float32),
        "heat_flow_ability": jnp.clip(jnp.exp(math.log(2.0) - 1.3862944 * jax.random.uniform(splits[1], (SHEET_NUMBER, SPAN_ALONG_X, SPAN_ALONG_Y), jnp.float32) ** levels(splits[1], (SHEET_NUMBER, SPAN_ALONG_X, SPAN_ALONG_Y), ((0, 2), (1, 16)), -0.2, 0.2)), 0.5, 2.0),
        "material_zone_label": touch_ends(jax.random.randint(splits[2], (SHEET_NUMBER, SPAN_ALONG_X, SPAN_ALONG_Y), 0, REGIONS), jax.random.fold_in(splits[2], 1), 0, REGIONS - 1).astype(jnp.int32),
        "reciprocal_warming_storage": jnp.clip(jnp.exp(jax.random.uniform(splits[3], (REGIONS,), jnp.float32, math.log(0.5), math.log(2.0))), 0.5, 2.0),
        "collector_potential_field": gaussian(splits[4], (SHEET_NUMBER, SPAN_ALONG_X, SPAN_ALONG_Y), 0.5, 4.0, ((0, 2), (1, 16)), jnp.float32),
        "tab_indicator": touch_ends((jax.random.randint(splits[5], (SPAN_ALONG_X, SPAN_ALONG_Y), 0, 16) < 1).astype(jnp.int32), jax.random.fold_in(splits[5], 1), 0, 1),
        "sheet_node_link_matrix": gaussian(splits[6], (E, SHEET_NUMBER), SHEET_NUMBER ** -0.5, 1.5, (), jnp.float32),
        "solution_salt_level": gaussian(splits[7], (E, SPAN_ALONG_X, SPAN_ALONG_Y), 1.0, 6.0, ((1, 16), (2, 2)), jnp.float32),
        "grain_shell_level": gaussian(splits[8], (S, E, SPAN_ALONG_X, SPAN_ALONG_Y), 1.0, 6.0, ((2, 16), (3, 2)), jnp.float32),
        "solution_diffusion_matrix": draw_solution_diffusion_matrix(jax.random.fold_in(splits[11], 71), 0),
        "grain_diffusion_matrix": draw_grain_diffusion_matrix(jax.random.fold_in(splits[11], 71), 0),
    }


warming_advance = 0.04
damping_weight = 4.5
imposed_excitation = 0.6
shell_flux = 0.5
film_resist = 0.5


def discrete_diffusion_stencil(field):
    padded_grid = jnp.pad(field, 1)
    neighbour_entries = padded_grid[2:, 1:-1, 1:-1] + padded_grid[:-2, 1:-1, 1:-1]
    neighbour_entries = neighbour_entries + padded_grid[1:-1, 2:, 1:-1] + padded_grid[1:-1, :-2, 1:-1]
    neighbour_entries = neighbour_entries + padded_grid[1:-1, 1:-1, 2:] + padded_grid[1:-1, 1:-1, :-2]
    return neighbour_entries - 6.0 * field


def flat_aggregate_result(field):
    padded_grid = jnp.pad(field, ((0, 0), (1, 1), (1, 1)))
    return padded_grid[:, 2:, 1:-1] + padded_grid[:, :-2, 1:-1] + padded_grid[:, 1:-1, 2:] + padded_grid[:, 1:-1, :-2]


def advance_stack_vertical(temp_col, volt_col, sheet_node_link_matrix, solution_salt_level, grain_shell_level, solution_diffusion_matrix, grain_diffusion_matrix):
    highest = lax.Precision.HIGHEST
    shells = grain_diffusion_matrix.shape[0]
    node_temp = jnp.einsum('el,lxy->exy', sheet_node_link_matrix, temp_col, precision=highest)
    node_voltage = jnp.einsum('el,lxy->exy', sheet_node_link_matrix, volt_col, precision=highest)
    next_solution_level = jnp.einsum('ef,fxy->exy', solution_diffusion_matrix, solution_salt_level, precision=highest)
    surface_base = jnp.einsum('s,sexy->exy', grain_diffusion_matrix[shells - 1], grain_shell_level, precision=highest)
    gain = shell_flux * grain_diffusion_matrix[shells - 1, shells - 1]
    rate = 0.5 * jax.nn.sigmoid(0.3 * node_temp) * jax.nn.sigmoid(next_solution_level)
    reaction = jnp.zeros_like(node_temp)
    for iteration in range(BV_ITERS):
        surface = surface_base - gain * reaction
        overvoltage = node_voltage - jnp.tanh(surface) - film_resist * reaction
        reaction = 2.0 * rate * jnp.sinh(0.5 * overvoltage)
    surface = surface_base - gain * reaction
    source = reaction * (node_voltage - jnp.tanh(surface))
    next_grain_level = jnp.einsum('st,texy->sexy', grain_diffusion_matrix, grain_shell_level, precision=highest)
    next_grain_level = next_grain_level - shell_flux * grain_diffusion_matrix[:, shells - 1][:, None, None, None] * reaction[None]
    reaction_warming_sheets = jnp.einsum('el,exy->lxy', sheet_node_link_matrix, source, precision=highest)
    reaction_flux_sheets = jnp.einsum('el,exy->lxy', sheet_node_link_matrix, reaction, precision=highest)
    return reaction_warming_sheets, reaction_flux_sheets, next_grain_level, next_solution_level


def reference(warmth_level, heat_flow_ability, material_zone_label, reciprocal_warming_storage, collector_potential_field, tab_indicator, sheet_node_link_matrix, solution_salt_level, grain_shell_level, solution_diffusion_matrix, grain_diffusion_matrix):
    stored_coulomb_limit = reciprocal_warming_storage[material_zone_label]
    next_warmth_level = warmth_level + warming_advance * stored_coulomb_limit * heat_flow_ability * discrete_diffusion_stencil(warmth_level)
    bounded_entries = (1 - tab_indicator).astype(jnp.float32)[None]
    battery_potential_drop = collector_potential_field
    for sweep in range(SWEEPS):
        battery_potential_drop = bounded_entries * (flat_aggregate_result(battery_potential_drop) + imposed_excitation * next_warmth_level) / damping_weight
    reaction_warming_sheets, reaction_flux_sheets, next_grain_level, next_solution_level = advance_stack_vertical(next_warmth_level, battery_potential_drop, sheet_node_link_matrix, solution_salt_level, grain_shell_level, solution_diffusion_matrix, grain_diffusion_matrix)
    return next_warmth_level, reaction_warming_sheets, reaction_flux_sheets, next_grain_level, next_solution_level
```

```python
import functools

import jax
import jax.numpy as jnp
from jax import lax
from jax.experimental import pallas as pl
from jax.experimental.pallas import tpu as pltpu
from jax.sharding import PartitionSpec as P

SWEEPS = 3
BV_ITERS = 4


warming_advance = 0.04
damping_weight = 4.5
imposed_excitation = 0.6
shell_flux = 0.5
film_resist = 0.5

LANES = 128
ROWS = 8
LOG2 = 0.6931471805599453
HIGHEST = lax.Precision.HIGHEST


def extended(block, sides, width):
    for axis, dim in sides:
        count = lax.axis_size(axis)
        forward = [(i, i + 1) for i in range(count - 1)]
        backward = [(target, source) for source, target in forward]
        low = lax.ppermute(
            lax.slice_in_dim(block, block.shape[dim] - width, None, axis=dim), axis, forward
        )
        high = lax.ppermute(lax.slice_in_dim(block, 0, width, axis=dim), axis, backward)
        block = jnp.concatenate([low, block, high], axis=dim)
    return block


def advance_stack_vertical(
    temp_col,
    volt_col,
    sheet_node_link_matrix,
    solution_salt_level,
    grain_shell_level,
    solution_diffusion_matrix,
    grain_diffusion_matrix,
):
    highest = lax.Precision.HIGHEST
    shells = grain_diffusion_matrix.shape[0]
    node_temp = jnp.einsum("el,lxy->exy", sheet_node_link_matrix, temp_col, precision=highest)
    node_voltage = jnp.einsum("el,lxy->exy", sheet_node_link_matrix, volt_col, precision=highest)
    next_solution_level = jnp.einsum(
        "ef,fxy->exy", solution_diffusion_matrix, solution_salt_level, precision=highest
    )
    surface_base = jnp.einsum(
        "s,sexy->exy", grain_diffusion_matrix[shells - 1], grain_shell_level, precision=highest
    )
    gain = shell_flux * grain_diffusion_matrix[shells - 1, shells - 1]
    rate = 0.5 * jax.nn.sigmoid(0.3 * node_temp) * jax.nn.sigmoid(next_solution_level)
    reaction = jnp.zeros_like(node_temp)
    for iteration in range(BV_ITERS):
        surface = surface_base - gain * reaction
        overvoltage = node_voltage - jnp.tanh(surface) - film_resist * reaction
        reaction = 2.0 * rate * jnp.sinh(0.5 * overvoltage)
    surface = surface_base - gain * reaction
    source = reaction * (node_voltage - jnp.tanh(surface))
    next_grain_level = jnp.einsum(
        "st,texy->sexy", grain_diffusion_matrix, grain_shell_level, precision=highest
    )
    next_grain_level = (
        next_grain_level
        - shell_flux * grain_diffusion_matrix[:, shells - 1][:, None, None, None] * reaction[None]
    )
    reaction_warming_sheets = jnp.einsum(
        "el,exy->lxy", sheet_node_link_matrix, source, precision=highest
    )
    reaction_flux_sheets = jnp.einsum(
        "el,exy->lxy", sheet_node_link_matrix, reaction, precision=highest
    )
    return (reaction_warming_sheets, reaction_flux_sheets, next_grain_level, next_solution_level)


def four_border_faces(bordered_lattice):
    return (
        bordered_lattice[:, 2:, 1:-1]
        + bordered_lattice[:, :-2, 1:-1]
        + bordered_lattice[:, 1:-1, 2:]
        + bordered_lattice[:, 1:-1, :-2]
    )


def per_device_general(
    warmth_level,
    heat_flow_ability,
    material_zone_label,
    reciprocal_warming_storage,
    collector_potential_field,
    tab_indicator,
    sheet_node_link_matrix,
    solution_salt_level,
    grain_shell_level,
    solution_diffusion_matrix,
    grain_diffusion_matrix,
):
    stored_coulomb_limit = jnp.zeros_like(warmth_level)
    for label in range(reciprocal_warming_storage.shape[0]):
        stored_coulomb_limit = stored_coulomb_limit + jnp.where(
            material_zone_label == label, reciprocal_warming_storage[label], 0.0
        )
    bordered_lattice = extended(warmth_level, (("tile", 1), ("layer", 0)), 1)
    bordered_lattice = jnp.pad(bordered_lattice, ((0, 0), (0, 0), (1, 1)))
    neighbour_entries = bordered_lattice[2:, 1:-1, 1:-1] + bordered_lattice[:-2, 1:-1, 1:-1]
    neighbour_entries = (
        neighbour_entries + bordered_lattice[1:-1, 2:, 1:-1] + bordered_lattice[1:-1, :-2, 1:-1]
    )
    neighbour_entries = (
        neighbour_entries + bordered_lattice[1:-1, 1:-1, 2:] + bordered_lattice[1:-1, 1:-1, :-2]
    )
    next_warmth_level = (
        warmth_level
        + warming_advance
        * stored_coulomb_limit
        * heat_flow_ability
        * (neighbour_entries - 6.0 * warmth_level)
    )
    bounded_entries = (1 - tab_indicator).astype(jnp.float32)[None]
    battery_potential_drop = collector_potential_field
    for sweep in range(SWEEPS):
        enclosed_lattice = extended(battery_potential_drop, (("tile", 1),), 1)
        enclosed_lattice = jnp.pad(enclosed_lattice, ((0, 0), (0, 0), (1, 1)))
        battery_potential_drop = (
            bounded_entries
            * (four_border_faces(enclosed_lattice) + imposed_excitation * next_warmth_level)
            / damping_weight
        )
    temp_col, volt_col = (
        lax.all_to_all(next_warmth_level, "layer", split_axis=2, concat_axis=0, tiled=True),
        lax.all_to_all(battery_potential_drop, "layer", split_axis=2, concat_axis=0, tiled=True),
    )
    heat_col, current_col, next_grain_level, next_solution_level = advance_stack_vertical(
        temp_col,
        volt_col,
        sheet_node_link_matrix,
        solution_salt_level,
        grain_shell_level,
        solution_diffusion_matrix,
        grain_diffusion_matrix,
    )
    reaction_warming_sheets, reaction_flux_sheets = (
        lax.all_to_all(heat_col, "layer", split_axis=0, concat_axis=2, tiled=True),
        lax.all_to_all(current_col, "layer", split_axis=0, concat_axis=2, tiled=True),
    )
    return (
        next_warmth_level,
        reaction_warming_sheets,
        reaction_flux_sheets,
        next_grain_level,
        next_solution_level,
    )


def along_span(field, blocks):
    rows = field.shape[0]
    lane = lax.broadcasted_iota(jnp.int32, field.shape, 1)
    block = lax.rem(lax.broadcasted_iota(jnp.int32, field.shape, 0), blocks)
    low = pltpu.roll(field, 1, 1)
    low_carry = jnp.where(block == 0, 0.0, pltpu.roll(low, 1, 0))
    high = pltpu.roll(field, LANES - 1, 1)
    high_carry = jnp.where(block == blocks - 1, 0.0, pltpu.roll(high, rows - 1, 0))
    return jnp.where(lane == 0, low_carry, low) + jnp.where(lane == LANES - 1, high_carry, high)


def along_sheets(field, blocks):
    rows = field.shape[0]
    row = lax.broadcasted_iota(jnp.int32, field.shape, 0)
    low = jnp.where(row < blocks, 0.0, pltpu.roll(field, blocks, 0))
    high = jnp.where(row >= rows - blocks, 0.0, pltpu.roll(field, rows - blocks, 0))
    return low + high


def fetch(pairs, sems):
    copies = [pltpu.make_async_copy(src, dst, sems.at[i]) for i, (src, dst) in enumerate(pairs)]
    for copy in copies:
        copy.start()
    return copies


def pack_kernel(
    blocks, storage, warmth, ability, zone, potential, tab, out, regions, heat, label, tabs, sems
):
    n = warmth.shape[0]
    copies = fetch(
        (
            (storage, regions),
            (zone, label),
            (ability, heat),
            (tab, tabs),
            (warmth, out.at[0:n]),
            (potential, out.at[n : 2 * n]),
        ),
        sems,
    )
    for copy in copies[:4]:
        copy.wait()
    zones = label[...]
    capacity = jnp.full(zones.shape, regions[0])
    for region in range(1, regions.shape[0]):
        capacity = jnp.where(zones == region, regions[region], capacity)
    out[2 * n : 3 * n, :] = warming_advance * capacity * heat[...]
    free = (1 - tabs[...]).astype(jnp.float32) * (1.0 / damping_weight)
    out[3 * n : 3 * n + blocks, :] = free
    out[3 * n + blocks : 3 * n + 2 * blocks, :] = free
    for copy in copies[4:]:
        copy.wait()


def spread(count, total, per):
    row = lax.broadcasted_iota(jnp.int32, (total, count), 0)
    column = lax.broadcasted_iota(jnp.int32, (total, count), 1)
    return (row // per == column).astype(jnp.float32)


def wide(matrix, per):
    rows, columns = matrix.shape
    left = spread(rows, rows * per, per)
    right = spread(columns, columns * per, per)
    full = jnp.dot(left, matrix, precision=HIGHEST, preferred_element_type=jnp.float32)
    full = lax.dot_general(
        full, right, (((1,), (1,)), ((), ())), precision=HIGHEST, preferred_element_type=jnp.float32
    )
    row = lax.broadcasted_iota(jnp.int32, full.shape, 0)
    column = lax.broadcasted_iota(jnp.int32, full.shape, 1)
    return jnp.where(lax.rem(row, per) == lax.rem(column, per), full, 0.0)


def halves(value):
    high = value.astype(jnp.bfloat16)
    return high, (value - high.astype(jnp.float32)).astype(jnp.bfloat16)


def local_kernel(
    diffusion, grain, salt, salt_matrix, held, local, weights, level, matrix, sems, grain_sems
):
    shells, nodes, _ = grain.shape
    part = shells // grain_sems.shape[0]
    small = fetch(((salt, level), (salt_matrix, matrix), (diffusion, weights)), sems)
    copies = fetch(
        [
            (grain.at[s : s + part], held.at[s : s + part])
            for s in range(0, shells, part)
        ],
        grain_sems,
    )
    for copy in small:
        copy.wait()
    local[nodes : 2 * nodes, :] = jnp.dot(
        wide(matrix[...], nodes // matrix.shape[0]),
        level[...],
        precision=HIGHEST,
        preferred_element_type=jnp.float32,
    )
    surface = jnp.zeros((nodes, LANES), jnp.float32)
    for i, copy in enumerate(copies):
        copy.wait()
        for shell in range(i * part, (i + 1) * part):
            surface = surface + weights[shells - 1, shell] * held[shell]
    local[0:nodes, :] = surface


def grain_kernel(grain, shells_matrix, base):
    shells, nodes, _ = grain.shape
    matrix_high, matrix_low = halves(wide(shells_matrix[...], ROWS))
    for start in range(0, nodes, 2 * ROWS):
        pair = [
            grain[:, start + k * ROWS : start + (k + 1) * ROWS, :].reshape(shells * ROWS, LANES)
            for k in range(2)
        ]
        high, low = halves(jnp.concatenate(pair, axis=1))
        dot = functools.partial(jnp.dot, preferred_element_type=jnp.float32)
        result = dot(matrix_high, high) + (dot(matrix_high, low) + dot(matrix_low, high))
        for k in range(2):
            part = result[:, k * LANES : (k + 1) * LANES].reshape(shells, ROWS, LANES)
            base[:, start + k * ROWS : start + (k + 1) * ROWS, :] = part


def sweep_kernel(sheets, blocks, tiles, local, own, partner, near, far, inner, out, masks):
    n = sheets * blocks
    size = own.shape[0]
    tile = lax.axis_index("tile")
    block = lax.axis_index("layer")
    first = jnp.logical_or(tile == 0, tile == tiles - 1)
    second = jnp.logical_or(tile == 2, tile == tiles - 3)
    beside = jnp.logical_or(tile == 1, tile == tiles - 2)
    keep_outer = jnp.where(first, 0.0, 1.0)
    keep_far = jnp.where(jnp.logical_or(first, second), 0.0, 1.0)
    keep_inner = jnp.where(beside, 0.0, 1.0)

    def load(ref, start, rows, keep=None):
        value = ref[start : start + rows, :]
        return value if keep is None else keep * value

    def window(start, rows):
        return [
            load(near, size + start, rows, keep_outer),
            load(near, start, rows, keep_outer),
            load(own, start, rows),
            load(partner, start, rows),
            load(inner, start, rows, keep_inner),
        ]

    warmth = [load(far, 0, n, keep_far)] + window(0, n) + [load(inner, size, n, keep_inner)]
    volt = [load(far, n, n, keep_far)] + window(n, n) + [load(inner, size + n, n, keep_inner)]
    slope = window(2 * n, n)
    free = window(3 * n, 2 * blocks)
    for i in range(5):
        masks[2 * i * blocks : 2 * (i + 1) * blocks, :] = free[i]
    free = [jnp.concatenate([m] * (n // m.shape[0]), axis=0) for m in free]
    temp = []
    for i in range(5):
        w = warmth[i + 1]
        around = warmth[i] + warmth[i + 2] + along_sheets(w, blocks) + along_span(w, blocks)
        temp.append(w + slope[i] * (around - 6.0 * w))
    for sweep in range(SWEEPS):
        volt = [
            free[i + sweep]
            * (
                volt[i]
                + volt[i + 2]
                + along_span(volt[i + 1], blocks)
                + imposed_excitation * temp[i + sweep]
            )
            for i in range(len(volt) - 2)
        ]
    out[0:n, :] = temp[2]
    out[n : 2 * n, :] = volt[0]
    for i in range(5):
        for k, value in enumerate((warmth[i + 1], slope[i])):
            edge = jnp.where(block == 0, value[n - blocks :, :], value[0:blocks, :])
            start = 2 * n + (2 * i + k) * blocks
            out[start : start + blocks, :] = edge
    out[2 * n + 10 * blocks :, :] = local[...]


def react(surface_base, gain, rate, node_voltage):
    reaction = jnp.zeros_like(node_voltage)
    for iteration in range(BV_ITERS):
        surface = surface_base - gain * reaction
        half = 0.5 * (node_voltage - jnp.tanh(surface) - film_resist * reaction)
        reaction = rate * (jnp.exp(half - LOG2) - jnp.exp(-half - LOG2))
    surface = surface_base - gain * reaction
    return reaction, reaction * (node_voltage - jnp.tanh(surface))


def reaction_kernel(
    sheets,
    blocks,
    diffusion,
    mine,
    other,
    masks,
    base,
    link,
    turned,
    next_warmth,
    warming,
    flux,
    grain_out,
    salt_out,
    weights,
    both,
    sheets_now,
    copy_out,
    sems,
    grain_sems,
):
    n = sheets * blocks
    shells, nodes, _ = base.shape
    block = lax.axis_index("layer")
    edge = 2 * blocks
    start = 2 * n + 5 * edge
    early = fetch(((diffusion, weights), (mine.at[start + nodes : start + 2 * nodes], salt_out)), sems)

    free = [masks[i * edge : (i + 1) * edge, :] for i in range(5)]
    added = []
    for i in range(5):
        at = 2 * n + i * edge
        added.append(pltpu.roll(mine[at : at + edge, :], blocks, 0) * other[at : at + edge, :])
    volt = [jnp.zeros_like(added[0])] * 7
    for sweep in range(SWEEPS):
        volt = [
            free[i + sweep]
            * (
                volt[i]
                + volt[i + 2]
                + along_span(volt[i + 1], blocks)
                + imposed_excitation * added[i + sweep]
            )
            for i in range(len(volt) - 2)
        ]
    here = pl.ds(pl.multiple_of(block * n, ROWS), n)
    there = pl.ds(pl.multiple_of((1 - block) * n, ROWS), n)
    both[here, 0:LANES] = mine[0:n, :]
    both[there, 0:LANES] = other[0:n, :]
    both[here, LANES:] = mine[n : 2 * n, :]
    both[there, LANES:] = other[n : 2 * n, :]
    extra = jnp.concatenate([added[2], volt[0]], axis=1)
    extra = jnp.where(block == 0, extra, pltpu.roll(extra, blocks, 0))
    both[n - blocks : n + blocks, :] += extra
    warmth_copy = pltpu.make_async_copy(both.at[here, 0:LANES], next_warmth, sems.at[2])
    warmth_copy.start()

    dot = functools.partial(jnp.dot, precision=HIGHEST, preferred_element_type=jnp.float32)
    node = dot(link[...], both[...])
    early[0].wait()
    gain = shell_flux * weights[shells - 1, shells - 1]
    results = []
    for part, ref in enumerate((mine, other)):
        rows = slice(part * nodes, (part + 1) * nodes)
        node_temp, node_voltage = node[rows, 0:LANES], node[rows, LANES:]
        surface_base = ref[start : start + nodes, :]
        salt = ref[start + nodes : start + 2 * nodes, :]
        rate = 1.0 / ((1.0 + jnp.exp(-0.3 * node_temp)) * (1.0 + jnp.exp(-salt)))
        results.append(react(surface_base, gain, rate, node_voltage))
        if part == 0:
            reaction = results[0][0]
            copies = []
            step = shells // grain_sems.shape[0]
            for first in range(0, shells, step):
                for shell in range(first, first + step):
                    factor = shell_flux * weights[shell, shells - 1]
                    copy_out[shell] = base[shell] - factor * reaction
                copies.append(
                    pltpu.make_async_copy(
                        copy_out.at[first : first + step],
                        grain_out.at[first : first + step],
                        grain_sems.at[first // step],
                    )
                )
                copies[-1].start()
    columns = jnp.concatenate([jnp.concatenate(r[::-1], axis=1) for r in results], axis=0)
    sheets_now[...] = dot(turned[...], columns)
    late = [
        pltpu.make_async_copy(sheets_now.at[:, 0:LANES], warming, sems.at[3]),
        pltpu.make_async_copy(sheets_now.at[:, LANES:], flux, sems.at[4]),
    ]
    for copy in late:
        copy.start()
    for copy in early[1:] + [warmth_copy] + copies + late:
        copy.wait()


def link_kernel(blocks, parts, link, turned, wide_link, wide_turned):
    nodes, sheets = link.shape
    per = blocks // parts
    own = sheets // parts
    rows, columns = nodes * blocks, sheets * blocks
    layer = lax.axis_index("layer")
    dot = functools.partial(jnp.dot, precision=HIGHEST, preferred_element_type=jnp.float32)

    def iota(shape):
        return [lax.broadcasted_iota(jnp.int32, shape, axis) for axis in range(2)]

    def fits(r, c):
        part = lax.rem(r // (nodes * per) + layer, parts)
        return lax.rem(c, blocks) == part * per + lax.rem(r, per)

    r, c = iota((rows, nodes))
    pick = (lax.rem(r, nodes * per) // per == c).astype(jnp.float32)
    r, c = iota((sheets, columns))
    split = (c // blocks == r).astype(jnp.float32)
    r, c = iota((rows, columns))
    wide_link[...] = jnp.where(fits(r, c), dot(dot(pick, link[...]), split), 0.0)
    r, c = iota((nodes, rows))
    pick = (lax.rem(c, nodes * per) // per == r).astype(jnp.float32)
    r, c = iota((own * blocks, sheets))
    split = (r // blocks + own * layer == c).astype(jnp.float32)
    r, c = iota((own * blocks, rows))
    wide_turned[...] = jnp.where(fits(c, r), dot(dot(split, turned[...]), pick), 0.0)


VMEM = pl.BlockSpec(memory_space=pltpu.VMEM)
SMEM = pl.BlockSpec(memory_space=pltpu.SMEM)
HBM = pl.BlockSpec(memory_space=pltpu.HBM)


def shaped(*shape):
    return jax.ShapeDtypeStruct(shape, jnp.float32)


def call(kernel, name, out, ins, outs, flops, nbytes, scratch=()):
    return pl.pallas_call(
        kernel,
        out_shape=out,
        in_specs=ins,
        out_specs=outs,
        scratch_shapes=scratch,
        compiler_params=pltpu.CompilerParams(vmem_limit_bytes=32 * 1024 * 1024),
        cost_estimate=pl.CostEstimate(flops=flops, bytes_accessed=nbytes, transcendentals=0),
        name=name,
    )


def per_device(
    tiles,
    warmth_level,
    heat_flow_ability,
    material_zone_label,
    reciprocal_warming_storage,
    collector_potential_field,
    tab_indicator,
    sheet_node_link_matrix,
    solution_salt_level,
    grain_shell_level,
    solution_diffusion_matrix,
    grain_diffusion_matrix,
):
    sheets, _, span = warmth_level.shape
    shells, points, _, part = grain_shell_level.shape
    blocks = span // LANES
    nodes = points * part // LANES
    n = sheets * blocks
    edge = 2 * blocks

    def both_layers(pairs):
        return [(s * 2 + j, t * 2 + j) for s, t in pairs for j in range(2)]

    def across(where):
        return [(t * 2 + j, t * 2 + 1 - j) for t in where for j in range(2)]

    def mutual(pairs):
        return pairs + [(t, s) for s, t in pairs]

    def send(value, pairs):
        return lax.ppermute(value, ("tile", "layer"), pairs)

    cores = both_layers(mutual([(t, t + 1) for t in range(0, tiles, 2)]))
    beside = both_layers(mutual([(t, t - 1) for t in range(2, tiles, 2)]))
    beside = beside + across([0, tiles - 1])
    beyond = both_layers(mutual([(t, t - 3) for t in range(4, tiles, 2)]))
    beyond = beyond + across([0, 2, tiles - 3, tiles - 1])
    layers = across(range(tiles))

    own = call(
        functools.partial(pack_kernel, blocks),
        "pack",
        shaped(3 * n + edge, LANES),
        [HBM] * 6,
        VMEM,
        1000,
        100000,
        (
            pltpu.SMEM(reciprocal_warming_storage.shape, jnp.float32),
            pltpu.VMEM((n, LANES), jnp.float32),
            pltpu.VMEM((n, LANES), jnp.int32),
            pltpu.VMEM((blocks, LANES), jnp.int32),
            pltpu.SemaphoreType.DMA((6,)),
        ),
    )(
        reciprocal_warming_storage,
        warmth_level.reshape(n, LANES),
        heat_flow_ability.reshape(n, LANES),
        material_zone_label.reshape(n, LANES),
        collector_potential_field.reshape(n, LANES),
        tab_indicator.reshape(blocks, LANES),
    )
    partner = send(own, cores)
    near = send(jnp.concatenate([own, partner], axis=0), beside)
    far = send(own[0 : 2 * n], beyond)
    held, local = call(
        local_kernel,
        "columns",
        (shaped(shells, nodes, LANES), shaped(2 * nodes, LANES)),
        [HBM] * 4,
        (VMEM, VMEM),
        10**7,
        3000000,
        (
            pltpu.SMEM(grain_diffusion_matrix.shape, jnp.float32),
            pltpu.VMEM((nodes, LANES), jnp.float32),
            pltpu.VMEM(solution_diffusion_matrix.shape, jnp.float32),
            pltpu.SemaphoreType.DMA((3,)),
            pltpu.SemaphoreType.DMA((4,)),
        ),
    )(
        grain_diffusion_matrix,
        grain_shell_level.reshape(shells, nodes, LANES),
        solution_salt_level.reshape(nodes, LANES),
        solution_diffusion_matrix,
    )
    near, far, held, local = lax.optimization_barrier((near, far, held, local))
    inner = send(near, cores)
    mine, masks = call(
        functools.partial(sweep_kernel, sheets, blocks, tiles),
        "sweeps",
        (shaped(2 * n + 5 * edge + 2 * nodes, LANES), shaped(5 * edge, LANES)),
        [VMEM] * 6,
        (VMEM, VMEM),
        10**6,
        500000,
    )(local, own, partner, near, far, inner)
    other = send(mine, layers)
    held, masks = lax.optimization_barrier((held, masks))
    base = call(
        grain_kernel,
        "grains",
        shaped(shells, nodes, LANES),
        [VMEM] * 2,
        VMEM,
        10**9,
        3000000,
    )(held, grain_diffusion_matrix)
    link, turned = call(
        functools.partial(link_kernel, blocks, 2),
        "links",
        (shaped(points * blocks, 2 * n), shaped(n, points * blocks)),
        [VMEM] * 2,
        (VMEM, VMEM),
        10**7,
        100000,
    )(sheet_node_link_matrix, sheet_node_link_matrix.T)
    next_warmth, warming, flux, grain, salt = call(
        functools.partial(reaction_kernel, sheets, blocks),
        "reaction",
        (
            shaped(n, LANES),
            shaped(n, LANES),
            shaped(n, LANES),
            shaped(shells, nodes, LANES),
            shaped(nodes, LANES),
        ),
        [HBM] + [VMEM] * 6,
        (HBM,) * 5,
        10**7,
        3000000,
        (
            pltpu.SMEM(grain_diffusion_matrix.shape, jnp.float32),
            pltpu.VMEM((2 * n, 2 * LANES), jnp.float32),
            pltpu.VMEM((n, 2 * LANES), jnp.float32),
            pltpu.VMEM((shells, nodes, LANES), jnp.float32),
            pltpu.SemaphoreType.DMA((5,)),
            pltpu.SemaphoreType.DMA((4,)),
        ),
    )(grain_diffusion_matrix, mine, other, masks, base, link, turned)
    return (
        next_warmth.reshape(warmth_level.shape),
        warming.reshape(warmth_level.shape),
        flux.reshape(warmth_level.shape),
        grain.reshape(grain_shell_level.shape),
        salt.reshape(solution_salt_level.shape),
    )


def solution(mesh):
    placed = (
        P("layer", "tile", None),
        P("layer", "tile", None),
        P("layer", "tile", None),
        P(),
        P("layer", "tile", None),
        P("tile", None),
        P(),
        P(None, "tile", "layer"),
        P(None, None, "tile", "layer"),
        P(),
        P(),
    )
    tiles, parts = mesh.shape["tile"], mesh.shape["layer"]
    plan = functools.partial(per_device, tiles) if parts == 2 else per_device_general
    return jax.shard_map(
        plan,
        mesh=mesh,
        in_specs=placed,
        out_specs=(
            P("layer", "tile", None),
            P("layer", "tile", None),
            P("layer", "tile", None),
            P(None, None, "tile", "layer"),
            P(None, "tile", "layer"),
        ),
        check_vma=False,
    )
```

```python
import functools

import jax
import jax.numpy as jnp
from jax import lax
from jax.experimental import pallas as pl
from jax.experimental.pallas import tpu as pltpu
from jax.sharding import PartitionSpec as P

SWEEPS = 3
BV_ITERS = 4


warming_advance = 0.04
damping_weight = 4.5
imposed_excitation = 0.6
shell_flux = 0.5
film_resist = 0.5

LANES = 128
ROWS = 8
LOG2 = 0.6931471805599453
HIGHEST = lax.Precision.HIGHEST


def extended(block, sides, width):
    for axis, dim in sides:
        count = lax.axis_size(axis)
        forward = [(i, i + 1) for i in range(count - 1)]
        backward = [(target, source) for source, target in forward]
        low = lax.ppermute(
            lax.slice_in_dim(block, block.shape[dim] - width, None, axis=dim), axis, forward
        )
        high = lax.ppermute(lax.slice_in_dim(block, 0, width, axis=dim), axis, backward)
        block = jnp.concatenate([low, block, high], axis=dim)
    return block


def advance_stack_vertical(
    temp_col,
    volt_col,
    sheet_node_link_matrix,
    solution_salt_level,
    grain_shell_level,
    solution_diffusion_matrix,
    grain_diffusion_matrix,
):
    highest = lax.Precision.HIGHEST
    shells = grain_diffusion_matrix.shape[0]
    node_temp = jnp.einsum("el,lxy->exy", sheet_node_link_matrix, temp_col, precision=highest)
    node_voltage = jnp.einsum("el,lxy->exy", sheet_node_link_matrix, volt_col, precision=highest)
    next_solution_level = jnp.einsum(
        "ef,fxy->exy", solution_diffusion_matrix, solution_salt_level, precision=highest
    )
    surface_base = jnp.einsum(
        "s,sexy->exy", grain_diffusion_matrix[shells - 1], grain_shell_level, precision=highest
    )
    gain = shell_flux * grain_diffusion_matrix[shells - 1, shells - 1]
    rate = 0.5 * jax.nn.sigmoid(0.3 * node_temp) * jax.nn.sigmoid(next_solution_level)
    reaction = jnp.zeros_like(node_temp)
    for iteration in range(BV_ITERS):
        surface = surface_base - gain * reaction
        overvoltage = node_voltage - jnp.tanh(surface) - film_resist * reaction
        reaction = 2.0 * rate * jnp.sinh(0.5 * overvoltage)
    surface = surface_base - gain * reaction
    source = reaction * (node_voltage - jnp.tanh(surface))
    next_grain_level = jnp.einsum(
        "st,texy->sexy", grain_diffusion_matrix, grain_shell_level, precision=highest
    )
    next_grain_level = (
        next_grain_level
        - shell_flux * grain_diffusion_matrix[:, shells - 1][:, None, None, None] * reaction[None]
    )
    reaction_warming_sheets = jnp.einsum(
        "el,exy->lxy", sheet_node_link_matrix, source, precision=highest
    )
    reaction_flux_sheets = jnp.einsum(
        "el,exy->lxy", sheet_node_link_matrix, reaction, precision=highest
    )
    return (reaction_warming_sheets, reaction_flux_sheets, next_grain_level, next_solution_level)


def four_border_faces(bordered_lattice):
    return (
        bordered_lattice[:, 2:, 1:-1]
        + bordered_lattice[:, :-2, 1:-1]
        + bordered_lattice[:, 1:-1, 2:]
        + bordered_lattice[:, 1:-1, :-2]
    )


def per_device_general(
    warmth_level,
    heat_flow_ability,
    material_zone_label,
    reciprocal_warming_storage,
    collector_potential_field,
    tab_indicator,
    sheet_node_link_matrix,
    solution_salt_level,
    grain_shell_level,
    solution_diffusion_matrix,
    grain_diffusion_matrix,
):
    stored_coulomb_limit = jnp.zeros_like(warmth_level)
    for label in range(reciprocal_warming_storage.shape[0]):
        stored_coulomb_limit = stored_coulomb_limit + jnp.where(
            material_zone_label == label, reciprocal_warming_storage[label], 0.0
        )
    bordered_lattice = extended(warmth_level, (("tile", 1), ("layer", 0)), 1)
    bordered_lattice = jnp.pad(bordered_lattice, ((0, 0), (0, 0), (1, 1)))
    neighbour_entries = bordered_lattice[2:, 1:-1, 1:-1] + bordered_lattice[:-2, 1:-1, 1:-1]
    neighbour_entries = (
        neighbour_entries + bordered_lattice[1:-1, 2:, 1:-1] + bordered_lattice[1:-1, :-2, 1:-1]
    )
    neighbour_entries = (
        neighbour_entries + bordered_lattice[1:-1, 1:-1, 2:] + bordered_lattice[1:-1, 1:-1, :-2]
    )
    next_warmth_level = (
        warmth_level
        + warming_advance
        * stored_coulomb_limit
        * heat_flow_ability
        * (neighbour_entries - 6.0 * warmth_level)
    )
    bounded_entries = (1 - tab_indicator).astype(jnp.float32)[None]
    battery_potential_drop = collector_potential_field
    for sweep in range(SWEEPS):
        enclosed_lattice = extended(battery_potential_drop, (("tile", 1),), 1)
        enclosed_lattice = jnp.pad(enclosed_lattice, ((0, 0), (0, 0), (1, 1)))
        battery_potential_drop = (
            bounded_entries
            * (four_border_faces(enclosed_lattice) + imposed_excitation * next_warmth_level)
            / damping_weight
        )
    temp_col, volt_col = (
        lax.all_to_all(next_warmth_level, "layer", split_axis=2, concat_axis=0, tiled=True),
        lax.all_to_all(battery_potential_drop, "layer", split_axis=2, concat_axis=0, tiled=True),
    )
    heat_col, current_col, next_grain_level, next_solution_level = advance_stack_vertical(
        temp_col,
        volt_col,
        sheet_node_link_matrix,
        solution_salt_level,
        grain_shell_level,
        solution_diffusion_matrix,
        grain_diffusion_matrix,
    )
    reaction_warming_sheets, reaction_flux_sheets = (
        lax.all_to_all(heat_col, "layer", split_axis=0, concat_axis=2, tiled=True),
        lax.all_to_all(current_col, "layer", split_axis=0, concat_axis=2, tiled=True),
    )
    return (
        next_warmth_level,
        reaction_warming_sheets,
        reaction_flux_sheets,
        next_grain_level,
        next_solution_level,
    )


def along_span(field, blocks):
    rows = field.shape[0]
    lane = lax.broadcasted_iota(jnp.int32, field.shape, 1)
    block = lax.rem(lax.broadcasted_iota(jnp.int32, field.shape, 0), blocks)
    low = pltpu.roll(field, 1, 1)
    low_carry = jnp.where(block == 0, 0.0, pltpu.roll(low, 1, 0))
    high = pltpu.roll(field, LANES - 1, 1)
    high_carry = jnp.where(block == blocks - 1, 0.0, pltpu.roll(high, rows - 1, 0))
    return jnp.where(lane == 0, low_carry, low) + jnp.where(lane == LANES - 1, high_carry, high)


def along_sheets(field, blocks):
    rows = field.shape[0]
    row = lax.broadcasted_iota(jnp.int32, field.shape, 0)
    low = jnp.where(row < blocks, 0.0, pltpu.roll(field, blocks, 0))
    high = jnp.where(row >= rows - blocks, 0.0, pltpu.roll(field, rows - blocks, 0))
    return low + high


def fetch(pairs, sems):
    copies = [pltpu.make_async_copy(src, dst, sems.at[i]) for i, (src, dst) in enumerate(pairs)]
    for copy in copies:
        copy.start()
    return copies


def pack_kernel(
    blocks, storage, warmth, ability, zone, potential, tab, out, regions, heat, label, tabs, sems
):
    n = warmth.shape[0]
    copies = fetch(
        (
            (storage, regions),
            (zone, label),
            (ability, heat),
            (tab, tabs),
            (warmth, out.at[0:n]),
            (potential, out.at[n : 2 * n]),
        ),
        sems,
    )
    for copy in copies[:4]:
        copy.wait()
    zones = label[...]
    capacity = jnp.full(zones.shape, regions[0])
    for region in range(1, regions.shape[0]):
        capacity = jnp.where(zones == region, regions[region], capacity)
    out[2 * n : 3 * n, :] = warming_advance * capacity * heat[...]
    free = (1 - tabs[...]).astype(jnp.float32) * (1.0 / damping_weight)
    out[3 * n : 3 * n + blocks, :] = free
    out[3 * n + blocks : 3 * n + 2 * blocks, :] = free
    for copy in copies[4:]:
        copy.wait()


def spread(count, total, per):
    row = lax.broadcasted_iota(jnp.int32, (total, count), 0)
    column = lax.broadcasted_iota(jnp.int32, (total, count), 1)
    return (row // per == column).astype(jnp.float32)


def wide(matrix, per):
    rows, columns = matrix.shape
    left = spread(rows, rows * per, per)
    right = spread(columns, columns * per, per)
    full = jnp.dot(left, matrix, precision=HIGHEST, preferred_element_type=jnp.float32)
    full = lax.dot_general(
        full, right, (((1,), (1,)), ((), ())), precision=HIGHEST, preferred_element_type=jnp.float32
    )
    row = lax.broadcasted_iota(jnp.int32, full.shape, 0)
    column = lax.broadcasted_iota(jnp.int32, full.shape, 1)
    return jnp.where(lax.rem(row, per) == lax.rem(column, per), full, 0.0)


def halves(value):
    high = value.astype(jnp.bfloat16)
    return high, (value - high.astype(jnp.float32)).astype(jnp.bfloat16)


def local_kernel(
    diffusion, grain, salt, salt_matrix, held, local, weights, level, matrix, sems, grain_sems
):
    shells, nodes, _ = grain.shape
    part = shells // grain_sems.shape[0]
    small = fetch(((salt, level), (salt_matrix, matrix), (diffusion, weights)), sems)
    copies = fetch(
        [
            (grain.at[s : s + part], held.at[s : s + part])
            for s in range(0, shells, part)
        ],
        grain_sems,
    )
    for copy in small:
        copy.wait()
    local[nodes : 2 * nodes, :] = jnp.dot(
        wide(matrix[...], nodes // matrix.shape[0]),
        level[...],
        precision=HIGHEST,
        preferred_element_type=jnp.float32,
    )
    surface = jnp.zeros((nodes, LANES), jnp.float32)
    for i, copy in enumerate(copies):
        copy.wait()
        for shell in range(i * part, (i + 1) * part):
            surface = surface + weights[shells - 1, shell] * held[shell]
    local[0:nodes, :] = surface


def grain_kernel(grain, shells_matrix, base):
    shells, nodes, _ = grain.shape
    matrix_high, matrix_low = halves(wide(shells_matrix[...], ROWS))
    for start in range(0, nodes, 2 * ROWS):
        pair = [
            grain[:, start + k * ROWS : start + (k + 1) * ROWS, :].reshape(shells * ROWS, LANES)
            for k in range(2)
        ]
        high, low = halves(jnp.concatenate(pair, axis=1))
        dot = functools.partial(jnp.dot, preferred_element_type=jnp.float32)
        result = dot(matrix_high, high) + (dot(matrix_high, low) + dot(matrix_low, high))
        for k in range(2):
            part = result[:, k * LANES : (k + 1) * LANES].reshape(shells, ROWS, LANES)
            base[:, start + k * ROWS : start + (k + 1) * ROWS, :] = part


def sweep_kernel(sheets, blocks, tiles, local, own, partner, near, far, inner, out, masks):
    n = sheets * blocks
    size = own.shape[0]
    tile = lax.axis_index("tile")
    block = lax.axis_index("layer")
    first = jnp.logical_or(tile == 0, tile == tiles - 1)
    second = jnp.logical_or(tile == 2, tile == tiles - 3)
    beside = jnp.logical_or(tile == 1, tile == tiles - 2)
    keep_outer = jnp.where(first, 0.0, 1.0)
    keep_far = jnp.where(jnp.logical_or(first, second), 0.0, 1.0)
    keep_inner = jnp.where(beside, 0.0, 1.0)

    def load(ref, start, rows, keep=None):
        value = ref[start : start + rows, :]
        return value if keep is None else keep * value

    def window(start, rows):
        return [
            load(near, size + start, rows, keep_outer),
            load(near, start, rows, keep_outer),
            load(own, start, rows),
            load(partner, start, rows),
            load(inner, start, rows, keep_inner),
        ]

    warmth = [load(far, 0, n, keep_far)] + window(0, n) + [load(inner, size, n, keep_inner)]
    volt = [load(far, n, n, keep_far)] + window(n, n) + [load(inner, size + n, n, keep_inner)]
    slope = window(2 * n, n)
    free = window(3 * n, 2 * blocks)
    for i in range(5):
        masks[2 * i * blocks : 2 * (i + 1) * blocks, :] = free[i]
    free = [jnp.concatenate([m] * (n // m.shape[0]), axis=0) for m in free]
    temp = []
    for i in range(5):
        w = warmth[i + 1]
        around = warmth[i] + warmth[i + 2] + along_sheets(w, blocks) + along_span(w, blocks)
        temp.append(w + slope[i] * (around - 6.0 * w))
    for sweep in range(SWEEPS):
        volt = [
            free[i + sweep]
            * (
                volt[i]
                + volt[i + 2]
                + along_span(volt[i + 1], blocks)
                + imposed_excitation * temp[i + sweep]
            )
            for i in range(len(volt) - 2)
        ]
    out[0:n, :] = temp[2]
    out[n : 2 * n, :] = volt[0]
    for i in range(5):
        for k, value in enumerate((warmth[i + 1], slope[i])):
            edge = jnp.where(block == 0, value[n - blocks :, :], value[0:blocks, :])
            start = 2 * n + (2 * i + k) * blocks
            out[start : start + blocks, :] = edge
    out[2 * n + 10 * blocks :, :] = local[...]


def react(surface_base, gain, rate, node_voltage):
    reaction = jnp.zeros_like(node_voltage)
    for iteration in range(BV_ITERS):
        surface = surface_base - gain * reaction
        half = 0.5 * (node_voltage - jnp.tanh(surface) - film_resist * reaction)
        reaction = rate * (jnp.exp(half - LOG2) - jnp.exp(-half - LOG2))
    surface = surface_base - gain * reaction
    return reaction, reaction * (node_voltage - jnp.tanh(surface))


def reaction_kernel(
    sheets,
    blocks,
    diffusion,
    mine,
    other,
    masks,
    base,
    link,
    turned,
    next_warmth,
    warming,
    flux,
    grain_out,
    salt_out,
    weights,
    both,
    sheets_now,
    copy_out,
    sems,
    grain_sems,
):
    n = sheets * blocks
    shells, nodes, _ = base.shape
    block = lax.axis_index("layer")
    edge = 2 * blocks
    start = 2 * n + 5 * edge
    early = fetch(((diffusion, weights), (mine.at[start + nodes : start + 2 * nodes], salt_out)), sems)

    free = [masks[i * edge : (i + 1) * edge, :] for i in range(5)]
    added = []
    for i in range(5):
        at = 2 * n + i * edge
        added.append(pltpu.roll(mine[at : at + edge, :], blocks, 0) * other[at : at + edge, :])
    volt = [jnp.zeros_like(added[0])] * 7
    for sweep in range(SWEEPS):
        volt = [
            free[i + sweep]
            * (
                volt[i]
                + volt[i + 2]
                + along_span(volt[i + 1], blocks)
                + imposed_excitation * added[i + sweep]
            )
            for i in range(len(volt) - 2)
        ]
    here = pl.ds(pl.multiple_of(block * n, ROWS), n)
    there = pl.ds(pl.multiple_of((1 - block) * n, ROWS), n)
    both[here, 0:LANES] = mine[0:n, :]
    both[there, 0:LANES] = other[0:n, :]
    both[here, LANES:] = mine[n : 2 * n, :]
    both[there, LANES:] = other[n : 2 * n, :]
    extra = jnp.concatenate([added[2], volt[0]], axis=1)
    extra = jnp.where(block == 0, extra, pltpu.roll(extra, blocks, 0))
    both[n - blocks : n + blocks, :] += extra
    warmth_copy = pltpu.make_async_copy(both.at[here, 0:LANES], next_warmth, sems.at[2])
    warmth_copy.start()

    dot = functools.partial(jnp.dot, precision=HIGHEST, preferred_element_type=jnp.float32)
    node = dot(link[...], both[...])
    early[0].wait()
    gain = shell_flux * weights[shells - 1, shells - 1]
    results = []
    for part, ref in enumerate((mine, other)):
        rows = slice(part * nodes, (part + 1) * nodes)
        node_temp, node_voltage = node[rows, 0:LANES], node[rows, LANES:]
        surface_base = ref[start : start + nodes, :]
        salt = ref[start + nodes : start + 2 * nodes, :]
        rate = 1.0 / ((1.0 + jnp.exp(-0.3 * node_temp)) * (1.0 + jnp.exp(-salt)))
        results.append(react(surface_base, gain, rate, node_voltage))
        if part == 0:
            reaction = results[0][0]
            copies = []
            step = shells // grain_sems.shape[0]
            for first in range(0, shells, step):
                for shell in range(first, first + step):
                    factor = shell_flux * weights[shell, shells - 1]
                    copy_out[shell] = base[shell] - factor * reaction
                copies.append(
                    pltpu.make_async_copy(
                        copy_out.at[first : first + step],
                        grain_out.at[first : first + step],
                        grain_sems.at[first // step],
                    )
                )
                copies[-1].start()
    columns = jnp.concatenate([jnp.concatenate(r[::-1], axis=1) for r in results], axis=0)
    sheets_now[...] = dot(turned[...], columns)
    late = [
        pltpu.make_async_copy(sheets_now.at[:, 0:LANES], warming, sems.at[3]),
        pltpu.make_async_copy(sheets_now.at[:, LANES:], flux, sems.at[4]),
    ]
    for copy in late:
        copy.start()
    for copy in early[1:] + [warmth_copy] + copies + late:
        copy.wait()


def link_kernel(blocks, parts, link, turned, wide_link, wide_turned):
    nodes, sheets = link.shape
    per = blocks // parts
    own = sheets // parts
    rows, columns = nodes * blocks, sheets * blocks
    layer = lax.axis_index("layer")
    dot = functools.partial(jnp.dot, precision=HIGHEST, preferred_element_type=jnp.float32)

    def iota(shape):
        return [lax.broadcasted_iota(jnp.int32, shape, axis) for axis in range(2)]

    def fits(r, c):
        part = lax.rem(r // (nodes * per) + layer, parts)
        return lax.rem(c, blocks) == part * per + lax.rem(r, per)

    r, c = iota((rows, nodes))
    pick = (lax.rem(r, nodes * per) // per == c).astype(jnp.float32)
    r, c = iota((sheets, columns))
    split = (c // blocks == r).astype(jnp.float32)
    r, c = iota((rows, columns))
    wide_link[...] = jnp.where(fits(r, c), dot(dot(pick, link[...]), split), 0.0)
    r, c = iota((nodes, rows))
    pick = (lax.rem(c, nodes * per) // per == r).astype(jnp.float32)
    r, c = iota((own * blocks, sheets))
    split = (r // blocks + own * layer == c).astype(jnp.float32)
    r, c = iota((own * blocks, rows))
    wide_turned[...] = jnp.where(fits(c, r), dot(dot(split, turned[...]), pick), 0.0)


VMEM = pl.BlockSpec(memory_space=pltpu.VMEM)
SMEM = pl.BlockSpec(memory_space=pltpu.SMEM)
HBM = pl.BlockSpec(memory_space=pltpu.HBM)


def in_hbm(*values):
    return [pltpu.with_memory_space_constraint(value, pltpu.HBM) for value in values]


def shaped(*shape):
    return jax.ShapeDtypeStruct(shape, jnp.float32)


def call(kernel, name, out, ins, outs, flops, nbytes, scratch=()):
    return pl.pallas_call(
        kernel,
        out_shape=out,
        in_specs=ins,
        out_specs=outs,
        scratch_shapes=scratch,
        compiler_params=pltpu.CompilerParams(vmem_limit_bytes=32 * 1024 * 1024),
        cost_estimate=pl.CostEstimate(flops=flops, bytes_accessed=nbytes, transcendentals=0),
        name=name,
    )


def per_device(
    tiles,
    warmth_level,
    heat_flow_ability,
    material_zone_label,
    reciprocal_warming_storage,
    collector_potential_field,
    tab_indicator,
    sheet_node_link_matrix,
    solution_salt_level,
    grain_shell_level,
    solution_diffusion_matrix,
    grain_diffusion_matrix,
):
    sheets, _, span = warmth_level.shape
    shells, points, _, part = grain_shell_level.shape
    blocks = span // LANES
    nodes = points * part // LANES
    n = sheets * blocks
    edge = 2 * blocks

    def both_layers(pairs):
        return [(s * 2 + j, t * 2 + j) for s, t in pairs for j in range(2)]

    def across(where):
        return [(t * 2 + j, t * 2 + 1 - j) for t in where for j in range(2)]

    def mutual(pairs):
        return pairs + [(t, s) for s, t in pairs]

    def send(value, pairs):
        return lax.ppermute(value, ("tile", "layer"), pairs)

    cores = both_layers(mutual([(t, t + 1) for t in range(0, tiles, 2)]))
    beside = both_layers(mutual([(t, t - 1) for t in range(2, tiles, 2)]))
    beside = beside + across([0, tiles - 1])
    beyond = both_layers(mutual([(t, t - 3) for t in range(4, tiles, 2)]))
    beyond = beyond + across([0, 2, tiles - 3, tiles - 1])
    layers = across(range(tiles))

    own = call(
        functools.partial(pack_kernel, blocks),
        "pack",
        shaped(3 * n + edge, LANES),
        [HBM] * 6,
        VMEM,
        1000,
        100000,
        (
            pltpu.SMEM(reciprocal_warming_storage.shape, jnp.float32),
            pltpu.VMEM((n, LANES), jnp.float32),
            pltpu.VMEM((n, LANES), jnp.int32),
            pltpu.VMEM((blocks, LANES), jnp.int32),
            pltpu.SemaphoreType.DMA((6,)),
        ),
    )(
        *in_hbm(
            reciprocal_warming_storage,
            warmth_level.reshape(n, LANES),
            heat_flow_ability.reshape(n, LANES),
            material_zone_label.reshape(n, LANES),
            collector_potential_field.reshape(n, LANES),
            tab_indicator.reshape(blocks, LANES),
        )
    )
    partner = send(own, cores)
    near = send(jnp.concatenate([own, partner], axis=0), beside)
    far = send(own[0 : 2 * n], beyond)
    held, local = call(
        local_kernel,
        "columns",
        (shaped(shells, nodes, LANES), shaped(2 * nodes, LANES)),
        [HBM] * 4,
        (VMEM, VMEM),
        10**7,
        3000000,
        (
            pltpu.SMEM(grain_diffusion_matrix.shape, jnp.float32),
            pltpu.VMEM((nodes, LANES), jnp.float32),
            pltpu.VMEM(solution_diffusion_matrix.shape, jnp.float32),
            pltpu.SemaphoreType.DMA((3,)),
            pltpu.SemaphoreType.DMA((4,)),
        ),
    )(
        *in_hbm(
            grain_diffusion_matrix,
            grain_shell_level.reshape(shells, nodes, LANES),
            solution_salt_level.reshape(nodes, LANES),
            solution_diffusion_matrix,
        )
    )
    near, far, held, local = lax.optimization_barrier((near, far, held, local))
    inner = send(near, cores)
    mine, masks = call(
        functools.partial(sweep_kernel, sheets, blocks, tiles),
        "sweeps",
        (shaped(2 * n + 5 * edge + 2 * nodes, LANES), shaped(5 * edge, LANES)),
        [VMEM] * 6,
        (VMEM, VMEM),
        10**6,
        500000,
    )(local, own, partner, near, far, inner)
    other = send(mine, layers)
    held, masks = lax.optimization_barrier((held, masks))
    base = call(
        grain_kernel,
        "grains",
        shaped(shells, nodes, LANES),
        [VMEM] * 2,
        VMEM,
        10**9,
        3000000,
    )(held, grain_diffusion_matrix)
    link, turned = call(
        functools.partial(link_kernel, blocks, 2),
        "links",
        (shaped(points * blocks, 2 * n), shaped(n, points * blocks)),
        [VMEM] * 2,
        (VMEM, VMEM),
        10**7,
        100000,
    )(sheet_node_link_matrix, sheet_node_link_matrix.T)
    next_warmth, warming, flux, grain, salt = call(
        functools.partial(reaction_kernel, sheets, blocks),
        "reaction",
        (
            shaped(n, LANES),
            shaped(n, LANES),
            shaped(n, LANES),
            shaped(shells, nodes, LANES),
            shaped(nodes, LANES),
        ),
        [HBM] + [VMEM] * 6,
        (HBM,) * 5,
        10**7,
        3000000,
        (
            pltpu.SMEM(grain_diffusion_matrix.shape, jnp.float32),
            pltpu.VMEM((2 * n, 2 * LANES), jnp.float32),
            pltpu.VMEM((n, 2 * LANES), jnp.float32),
            pltpu.VMEM((shells, nodes, LANES), jnp.float32),
            pltpu.SemaphoreType.DMA((5,)),
            pltpu.SemaphoreType.DMA((4,)),
        ),
    )(*in_hbm(grain_diffusion_matrix), mine, other, masks, base, link, turned)
    return (
        next_warmth.reshape(warmth_level.shape),
        warming.reshape(warmth_level.shape),
        flux.reshape(warmth_level.shape),
        grain.reshape(grain_shell_level.shape),
        salt.reshape(solution_salt_level.shape),
    )


def solution(mesh):
    placed = (
        P("layer", "tile", None),
        P("layer", "tile", None),
        P("layer", "tile", None),
        P(),
        P("layer", "tile", None),
        P("tile", None),
        P(),
        P(None, "tile", "layer"),
        P(None, None, "tile", "layer"),
        P(),
        P(),
    )
    tiles, parts = mesh.shape["tile"], mesh.shape["layer"]
    plan = functools.partial(per_device, tiles) if parts == 2 else per_device_general
    return jax.shard_map(
        plan,
        mesh=mesh,
        in_specs=placed,
        out_specs=(
            P("layer", "tile", None),
            P("layer", "tile", None),
            P("layer", "tile", None),
            P(None, None, "tile", "layer"),
            P(None, "tile", "layer"),
        ),
        check_vma=False,
    )
```

```python
import functools

import jax
import jax.numpy as jnp
from jax import lax
from jax.experimental import pallas as pl
from jax.experimental.pallas import tpu as pltpu
from jax.sharding import PartitionSpec as P

SWEEPS = 3
BV_ITERS = 4


warming_advance = 0.04
damping_weight = 4.5
imposed_excitation = 0.6
shell_flux = 0.5
film_resist = 0.5

LANES = 128
ROWS = 8
LOG2 = 0.6931471805599453
HIGHEST = lax.Precision.HIGHEST


def extended(block, sides, width):
    for axis, dim in sides:
        count = lax.axis_size(axis)
        forward = [(i, i + 1) for i in range(count - 1)]
        backward = [(target, source) for source, target in forward]
        low = lax.ppermute(
            lax.slice_in_dim(block, block.shape[dim] - width, None, axis=dim), axis, forward
        )
        high = lax.ppermute(lax.slice_in_dim(block, 0, width, axis=dim), axis, backward)
        block = jnp.concatenate([low, block, high], axis=dim)
    return block


def advance_stack_vertical(
    temp_col,
    volt_col,
    sheet_node_link_matrix,
    solution_salt_level,
    grain_shell_level,
    solution_diffusion_matrix,
    grain_diffusion_matrix,
):
    highest = lax.Precision.HIGHEST
    shells = grain_diffusion_matrix.shape[0]
    node_temp = jnp.einsum("el,lxy->exy", sheet_node_link_matrix, temp_col, precision=highest)
    node_voltage = jnp.einsum("el,lxy->exy", sheet_node_link_matrix, volt_col, precision=highest)
    next_solution_level = jnp.einsum(
        "ef,fxy->exy", solution_diffusion_matrix, solution_salt_level, precision=highest
    )
    surface_base = jnp.einsum(
        "s,sexy->exy", grain_diffusion_matrix[shells - 1], grain_shell_level, precision=highest
    )
    gain = shell_flux * grain_diffusion_matrix[shells - 1, shells - 1]
    rate = 0.5 * jax.nn.sigmoid(0.3 * node_temp) * jax.nn.sigmoid(next_solution_level)
    reaction = jnp.zeros_like(node_temp)
    for iteration in range(BV_ITERS):
        surface = surface_base - gain * reaction
        overvoltage = node_voltage - jnp.tanh(surface) - film_resist * reaction
        reaction = 2.0 * rate * jnp.sinh(0.5 * overvoltage)
    surface = surface_base - gain * reaction
    source = reaction * (node_voltage - jnp.tanh(surface))
    next_grain_level = jnp.einsum(
        "st,texy->sexy", grain_diffusion_matrix, grain_shell_level, precision=highest
    )
    next_grain_level = (
        next_grain_level
        - shell_flux * grain_diffusion_matrix[:, shells - 1][:, None, None, None] * reaction[None]
    )
    reaction_warming_sheets = jnp.einsum(
        "el,exy->lxy", sheet_node_link_matrix, source, precision=highest
    )
    reaction_flux_sheets = jnp.einsum(
        "el,exy->lxy", sheet_node_link_matrix, reaction, precision=highest
    )
    return (reaction_warming_sheets, reaction_flux_sheets, next_grain_level, next_solution_level)


def four_border_faces(bordered_lattice):
    return (
        bordered_lattice[:, 2:, 1:-1]
        + bordered_lattice[:, :-2, 1:-1]
        + bordered_lattice[:, 1:-1, 2:]
        + bordered_lattice[:, 1:-1, :-2]
    )


def per_device_general(
    warmth_level,
    heat_flow_ability,
    material_zone_label,
    reciprocal_warming_storage,
    collector_potential_field,
    tab_indicator,
    sheet_node_link_matrix,
    solution_salt_level,
    grain_shell_level,
    solution_diffusion_matrix,
    grain_diffusion_matrix,
):
    stored_coulomb_limit = jnp.zeros_like(warmth_level)
    for label in range(reciprocal_warming_storage.shape[0]):
        stored_coulomb_limit = stored_coulomb_limit + jnp.where(
            material_zone_label == label, reciprocal_warming_storage[label], 0.0
        )
    bordered_lattice = extended(warmth_level, (("tile", 1), ("layer", 0)), 1)
    bordered_lattice = jnp.pad(bordered_lattice, ((0, 0), (0, 0), (1, 1)))
    neighbour_entries = bordered_lattice[2:, 1:-1, 1:-1] + bordered_lattice[:-2, 1:-1, 1:-1]
    neighbour_entries = (
        neighbour_entries + bordered_lattice[1:-1, 2:, 1:-1] + bordered_lattice[1:-1, :-2, 1:-1]
    )
    neighbour_entries = (
        neighbour_entries + bordered_lattice[1:-1, 1:-1, 2:] + bordered_lattice[1:-1, 1:-1, :-2]
    )
    next_warmth_level = (
        warmth_level
        + warming_advance
        * stored_coulomb_limit
        * heat_flow_ability
        * (neighbour_entries - 6.0 * warmth_level)
    )
    bounded_entries = (1 - tab_indicator).astype(jnp.float32)[None]
    battery_potential_drop = collector_potential_field
    for sweep in range(SWEEPS):
        enclosed_lattice = extended(battery_potential_drop, (("tile", 1),), 1)
        enclosed_lattice = jnp.pad(enclosed_lattice, ((0, 0), (0, 0), (1, 1)))
        battery_potential_drop = (
            bounded_entries
            * (four_border_faces(enclosed_lattice) + imposed_excitation * next_warmth_level)
            / damping_weight
        )
    temp_col, volt_col = (
        lax.all_to_all(next_warmth_level, "layer", split_axis=2, concat_axis=0, tiled=True),
        lax.all_to_all(battery_potential_drop, "layer", split_axis=2, concat_axis=0, tiled=True),
    )
    heat_col, current_col, next_grain_level, next_solution_level = advance_stack_vertical(
        temp_col,
        volt_col,
        sheet_node_link_matrix,
        solution_salt_level,
        grain_shell_level,
        solution_diffusion_matrix,
        grain_diffusion_matrix,
    )
    reaction_warming_sheets, reaction_flux_sheets = (
        lax.all_to_all(heat_col, "layer", split_axis=0, concat_axis=2, tiled=True),
        lax.all_to_all(current_col, "layer", split_axis=0, concat_axis=2, tiled=True),
    )
    return (
        next_warmth_level,
        reaction_warming_sheets,
        reaction_flux_sheets,
        next_grain_level,
        next_solution_level,
    )


def along_span(field, blocks):
    rows = field.shape[0]
    lane = lax.broadcasted_iota(jnp.int32, field.shape, 1)
    block = lax.rem(lax.broadcasted_iota(jnp.int32, field.shape, 0), blocks)
    low = pltpu.roll(field, 1, 1)
    low_carry = jnp.where(block == 0, 0.0, pltpu.roll(low, 1, 0))
    high = pltpu.roll(field, LANES - 1, 1)
    high_carry = jnp.where(block == blocks - 1, 0.0, pltpu.roll(high, rows - 1, 0))
    return jnp.where(lane == 0, low_carry, low) + jnp.where(lane == LANES - 1, high_carry, high)


def along_sheets(field, blocks):
    rows = field.shape[0]
    row = lax.broadcasted_iota(jnp.int32, field.shape, 0)
    low = jnp.where(row < blocks, 0.0, pltpu.roll(field, blocks, 0))
    high = jnp.where(row >= rows - blocks, 0.0, pltpu.roll(field, rows - blocks, 0))
    return low + high


def fetch(pairs, sems):
    copies = [pltpu.make_async_copy(src, dst, sems.at[i]) for i, (src, dst) in enumerate(pairs)]
    for copy in copies:
        copy.start()
    return copies


def pack_kernel(
    blocks, storage, warmth, ability, zone, potential, tab, out, regions, heat, label, tabs, sems
):
    n = warmth.shape[0]
    copies = fetch(
        (
            (storage, regions),
            (zone, label),
            (ability, heat),
            (tab, tabs),
            (warmth, out.at[0:n]),
            (potential, out.at[n : 2 * n]),
        ),
        sems,
    )
    for copy in copies[:4]:
        copy.wait()
    zones = label[...]
    capacity = jnp.full(zones.shape, regions[0])
    for region in range(1, regions.shape[0]):
        capacity = jnp.where(zones == region, regions[region], capacity)
    out[2 * n : 3 * n, :] = warming_advance * capacity * heat[...]
    free = (1 - tabs[...]).astype(jnp.float32) * (1.0 / damping_weight)
    out[3 * n : 3 * n + blocks, :] = free
    out[3 * n + blocks : 3 * n + 2 * blocks, :] = free
    for copy in copies[4:]:
        copy.wait()


def spread(count, total, per):
    row = lax.broadcasted_iota(jnp.int32, (total, count), 0)
    column = lax.broadcasted_iota(jnp.int32, (total, count), 1)
    return (row // per == column).astype(jnp.float32)


def wide(matrix, per):
    rows, columns = matrix.shape
    left = spread(rows, rows * per, per)
    right = spread(columns, columns * per, per)
    full = jnp.dot(left, matrix, precision=HIGHEST, preferred_element_type=jnp.float32)
    full = lax.dot_general(
        full, right, (((1,), (1,)), ((), ())), precision=HIGHEST, preferred_element_type=jnp.float32
    )
    row = lax.broadcasted_iota(jnp.int32, full.shape, 0)
    column = lax.broadcasted_iota(jnp.int32, full.shape, 1)
    return jnp.where(lax.rem(row, per) == lax.rem(column, per), full, 0.0)


def halves(value):
    high = value.astype(jnp.bfloat16)
    return high, (value - high.astype(jnp.float32)).astype(jnp.bfloat16)


def link_matrices(blocks, parts, turned, links, wide_link, wide_turned):
    sheets, points = turned.shape
    per = blocks // parts
    own = sheets // parts
    rows, columns = points * blocks, sheets * blocks
    layer = lax.axis_index("layer")
    product = functools.partial(
        lax.dot_general, precision=HIGHEST, preferred_element_type=jnp.float32
    )
    plain, across = (((1,), (0,)), ((), ())), (((1,), (1,)), ((), ()))

    def iota(shape):
        return [lax.broadcasted_iota(jnp.int32, shape, axis) for axis in range(2)]

    def fits(r, c):
        part = lax.rem(r // (points * per) + layer, parts)
        return lax.rem(c, blocks) == part * per + lax.rem(r, per)

    r, c = iota((rows, points))
    pick = (lax.rem(r, points * per) // per == c).astype(jnp.float32)
    r, c = iota((sheets, columns))
    split = (c // blocks == r).astype(jnp.float32)
    full = product(product(pick, links[...], across), split, plain)
    r, c = iota((rows, columns))
    wide_link[...] = jnp.where(fits(r, c), full, 0.0)
    r, c = iota((own * blocks, sheets))
    split = (r // blocks + own * layer == c).astype(jnp.float32)
    full = product(product(split, links[...], plain), pick, across)
    r, c = iota((own * blocks, rows))
    wide_turned[...] = jnp.where(fits(c, r), full, 0.0)


def local_kernel(
    blocks,
    parts,
    diffusion,
    grain,
    salt,
    salt_matrix,
    turned,
    held,
    local,
    wide_link,
    wide_turned,
    factors,
    weights,
    level,
    matrix,
    links,
    sems,
    grain_sems,
):
    shells, nodes, _ = grain.shape
    part = shells // grain_sems.shape[0]
    small = fetch(
        ((salt, level), (salt_matrix, matrix), (diffusion, weights), (turned, links)), sems
    )
    copies = fetch(
        [(grain.at[s : s + part], held.at[s : s + part]) for s in range(0, shells, part)],
        grain_sems,
    )
    for copy in small:
        copy.wait()
    local[nodes : 2 * nodes, :] = jnp.dot(
        wide(matrix[...], nodes // matrix.shape[0]),
        level[...],
        precision=HIGHEST,
        preferred_element_type=jnp.float32,
    )
    link_matrices(blocks, parts, turned, links, wide_link, wide_turned)
    for shell in range(shells):
        factors[shell : shell + 1, :] = jnp.full(
            (1, LANES), shell_flux * weights[shell, shells - 1]
        )
    surface = jnp.zeros((nodes, LANES), jnp.float32)
    for i, copy in enumerate(copies):
        copy.wait()
        for shell in range(i * part, (i + 1) * part):
            surface = surface + weights[shells - 1, shell] * held[shell]
    local[0:nodes, :] = surface


def grain_kernel(grain, weights, base):
    shells, count, _ = grain.shape
    matrix_high, matrix_low = halves(wide(weights[...], ROWS))
    for start in range(0, count, 2 * ROWS):
        pair = [
            grain[:, start + k * ROWS : start + (k + 1) * ROWS, :].reshape(shells * ROWS, LANES)
            for k in range(2)
        ]
        high, low = halves(jnp.concatenate(pair, axis=1))
        dot = functools.partial(jnp.dot, preferred_element_type=jnp.float32)
        result = dot(matrix_high, high) + (dot(matrix_high, low) + dot(matrix_low, high))
        for k in range(2):
            part = result[:, k * LANES : (k + 1) * LANES].reshape(shells, ROWS, LANES)
            base[:, start + k * ROWS : start + (k + 1) * ROWS, :] = part


def sweep_kernel(sheets, blocks, tiles, own, partner, near, far, inner, out, masks):
    n = sheets * blocks
    size = own.shape[0]
    tile = lax.axis_index("tile")
    block = lax.axis_index("layer")
    first = jnp.logical_or(tile == 0, tile == tiles - 1)
    second = jnp.logical_or(tile == 2, tile == tiles - 3)
    beside = jnp.logical_or(tile == 1, tile == tiles - 2)
    keep_outer = jnp.where(first, 0.0, 1.0)
    keep_far = jnp.where(jnp.logical_or(first, second), 0.0, 1.0)
    keep_inner = jnp.where(beside, 0.0, 1.0)

    def load(ref, start, rows, keep=None):
        value = ref[start : start + rows, :]
        return value if keep is None else keep * value

    def window(start, rows):
        return [
            load(near, size + start, rows, keep_outer),
            load(near, start, rows, keep_outer),
            load(own, start, rows),
            load(partner, start, rows),
            load(inner, start, rows, keep_inner),
        ]

    warmth = [load(far, 0, n, keep_far)] + window(0, n) + [load(inner, size, n, keep_inner)]
    volt = [load(far, n, n, keep_far)] + window(n, n) + [load(inner, size + n, n, keep_inner)]
    slope = window(2 * n, n)
    free = window(3 * n, 2 * blocks)
    for i in range(5):
        masks[2 * i * blocks : 2 * (i + 1) * blocks, :] = free[i]
    free = [jnp.concatenate([m] * (n // m.shape[0]), axis=0) for m in free]
    temp = []
    for i in range(5):
        w = warmth[i + 1]
        around = warmth[i] + warmth[i + 2] + along_sheets(w, blocks) + along_span(w, blocks)
        temp.append(w + slope[i] * (around - 6.0 * w))
    for sweep in range(SWEEPS):
        volt = [
            free[i + sweep]
            * (
                volt[i]
                + volt[i + 2]
                + along_span(volt[i + 1], blocks)
                + imposed_excitation * temp[i + sweep]
            )
            for i in range(len(volt) - 2)
        ]
    out[0:n, :] = temp[2]
    out[n : 2 * n, :] = volt[0]
    for i in range(5):
        for k, value in enumerate((warmth[i + 1], slope[i])):
            edge = jnp.where(block == 0, value[n - blocks :, :], value[0:blocks, :])
            start = 2 * n + (2 * i + k) * blocks
            out[start : start + blocks, :] = edge


def react(surface_base, gain, rate, node_voltage):
    reaction = jnp.zeros_like(node_voltage)
    for iteration in range(BV_ITERS):
        surface = surface_base - gain * reaction
        half = 0.5 * (node_voltage - jnp.tanh(surface) - film_resist * reaction)
        reaction = rate * (jnp.exp(half - LOG2) - jnp.exp(-half - LOG2))
    surface = surface_base - gain * reaction
    return reaction, reaction * (node_voltage - jnp.tanh(surface))


def reaction_kernel(
    sheets,
    blocks,
    factors,
    mine,
    other,
    local,
    other_local,
    masks,
    base,
    link,
    turned,
    next_warmth,
    warming,
    flux,
    grain_out,
    salt_out,
    both,
    sheets_now,
    copy_out,
    sems,
    grain_sems,
):
    n = sheets * blocks
    shells, nodes, _ = base.shape
    block = lax.axis_index("layer")
    edge = 2 * blocks
    early = fetch(((local.at[nodes : 2 * nodes], salt_out),), sems)

    free = [masks[i * edge : (i + 1) * edge, :] for i in range(5)]
    added = []
    for i in range(5):
        at = 2 * n + i * edge
        added.append(pltpu.roll(mine[at : at + edge, :], blocks, 0) * other[at : at + edge, :])
    volt = [jnp.zeros_like(added[0])] * 7
    for sweep in range(SWEEPS):
        volt = [
            free[i + sweep]
            * (
                volt[i]
                + volt[i + 2]
                + along_span(volt[i + 1], blocks)
                + imposed_excitation * added[i + sweep]
            )
            for i in range(len(volt) - 2)
        ]
    here = pl.ds(pl.multiple_of(block * n, ROWS), n)
    there = pl.ds(pl.multiple_of((1 - block) * n, ROWS), n)
    both[here, 0:LANES] = mine[0:n, :]
    both[there, 0:LANES] = other[0:n, :]
    both[here, LANES:] = mine[n : 2 * n, :]
    both[there, LANES:] = other[n : 2 * n, :]
    extra = jnp.concatenate([added[2], volt[0]], axis=1)
    extra = jnp.where(block == 0, extra, pltpu.roll(extra, blocks, 0))
    both[n - blocks : n + blocks, :] += extra
    warmth_copy = pltpu.make_async_copy(both.at[here, 0:LANES], next_warmth, sems.at[1])
    warmth_copy.start()

    dot = functools.partial(jnp.dot, precision=HIGHEST, preferred_element_type=jnp.float32)
    node = dot(link[...], both[...])
    gain = factors[shells - 1 :, :]
    surface_base = jnp.concatenate([local[0:nodes, :], other_local[0:nodes, :]], axis=0)
    salt = jnp.concatenate([local[nodes:, :], other_local[nodes:, :]], axis=0)
    rate = 1.0 / ((1.0 + jnp.exp(-0.3 * node[:, 0:LANES])) * (1.0 + jnp.exp(-salt)))
    reaction, source = react(surface_base, gain, rate, node[:, LANES:])
    sheets_now[...] = dot(turned[...], jnp.concatenate([source, reaction], axis=1))
    late = [
        pltpu.make_async_copy(sheets_now.at[:, 0:LANES], warming, sems.at[2]),
        pltpu.make_async_copy(sheets_now.at[:, LANES:], flux, sems.at[3]),
    ]
    for copy in late:
        copy.start()
    copies = []
    step = shells // grain_sems.shape[0]
    for first in range(0, shells, step):
        for shell in range(first, first + step):
            factor = factors[shell : shell + 1, :]
            copy_out[shell] = base[shell] - factor * reaction[0:nodes, :]
        copies.append(
            pltpu.make_async_copy(
                copy_out.at[first : first + step],
                grain_out.at[first : first + step],
                grain_sems.at[first // step],
            )
        )
        copies[-1].start()
    for copy in early + [warmth_copy] + copies + late:
        copy.wait()


VMEM = pl.BlockSpec(memory_space=pltpu.VMEM)
SMEM = pl.BlockSpec(memory_space=pltpu.SMEM)
HBM = pl.BlockSpec(memory_space=pltpu.HBM)


def in_hbm(*values):
    return [pltpu.with_memory_space_constraint(value, pltpu.HBM) for value in values]


def shaped(*shape):
    return jax.ShapeDtypeStruct(shape, jnp.float32)


def call(kernel, name, out, ins, outs, flops, nbytes, scratch=()):
    return pl.pallas_call(
        kernel,
        out_shape=out,
        in_specs=ins,
        out_specs=outs,
        scratch_shapes=scratch,
        compiler_params=pltpu.CompilerParams(vmem_limit_bytes=32 * 1024 * 1024),
        cost_estimate=pl.CostEstimate(flops=flops, bytes_accessed=nbytes, transcendentals=0),
        name=name,
    )


def per_device(
    tiles,
    warmth_level,
    heat_flow_ability,
    material_zone_label,
    reciprocal_warming_storage,
    collector_potential_field,
    tab_indicator,
    sheet_node_link_matrix,
    solution_salt_level,
    grain_shell_level,
    solution_diffusion_matrix,
    grain_diffusion_matrix,
):
    sheets, _, span = warmth_level.shape
    shells, points, _, part = grain_shell_level.shape
    blocks = span // LANES
    nodes = points * part // LANES
    n = sheets * blocks
    edge = 2 * blocks

    def both_layers(pairs):
        return [(s * 2 + j, t * 2 + j) for s, t in pairs for j in range(2)]

    def across(where):
        return [(t * 2 + j, t * 2 + 1 - j) for t in where for j in range(2)]

    def mutual(pairs):
        return pairs + [(t, s) for s, t in pairs]

    def send(value, pairs):
        return lax.ppermute(value, ("tile", "layer"), pairs)

    cores = both_layers(mutual([(t, t + 1) for t in range(0, tiles, 2)]))
    beside = both_layers(mutual([(t, t - 1) for t in range(2, tiles, 2)]))
    beside = beside + across([0, tiles - 1])
    beyond = both_layers(mutual([(t, t - 3) for t in range(4, tiles, 2)]))
    beyond = beyond + across([0, 2, tiles - 3, tiles - 1])
    layers = across(range(tiles))

    own = call(
        functools.partial(pack_kernel, blocks),
        "pack",
        shaped(3 * n + edge, LANES),
        [HBM] * 6,
        VMEM,
        1000,
        100000,
        (
            pltpu.SMEM(reciprocal_warming_storage.shape, jnp.float32),
            pltpu.VMEM((n, LANES), jnp.float32),
            pltpu.VMEM((n, LANES), jnp.int32),
            pltpu.VMEM((blocks, LANES), jnp.int32),
            pltpu.SemaphoreType.DMA((6,)),
        ),
    )(
        *in_hbm(
            reciprocal_warming_storage,
            warmth_level.reshape(n, LANES),
            heat_flow_ability.reshape(n, LANES),
            material_zone_label.reshape(n, LANES),
            collector_potential_field.reshape(n, LANES),
            tab_indicator.reshape(blocks, LANES),
        )
    )
    partner = send(own, cores)
    near = send(jnp.concatenate([own, partner], axis=0), beside)
    far = send(own[0 : 2 * n], beyond)
    held, local, link, turned, factors = call(
        functools.partial(local_kernel, blocks, 2),
        "columns",
        (
            shaped(shells, nodes, LANES),
            shaped(2 * nodes, LANES),
            shaped(points * blocks, 2 * n),
            shaped(n, points * blocks),
            shaped(shells, LANES),
        ),
        [HBM] * 5,
        (VMEM,) * 5,
        10**7,
        3000000,
        (
            pltpu.SMEM(grain_diffusion_matrix.shape, jnp.float32),
            pltpu.VMEM((nodes, LANES), jnp.float32),
            pltpu.VMEM(solution_diffusion_matrix.shape, jnp.float32),
            pltpu.VMEM(sheet_node_link_matrix.shape[::-1], jnp.float32),
            pltpu.SemaphoreType.DMA((4,)),
            pltpu.SemaphoreType.DMA((4,)),
        ),
    )(
        *in_hbm(
            grain_diffusion_matrix,
            grain_shell_level.reshape(shells, nodes, LANES),
            solution_salt_level.reshape(nodes, LANES),
            solution_diffusion_matrix,
            sheet_node_link_matrix.T,
        )
    )
    other_local = send(local, layers)
    near, far, held, local = lax.optimization_barrier((near, far, held, local))
    inner = send(near, cores)
    mine, masks = call(
        functools.partial(sweep_kernel, sheets, blocks, tiles),
        "sweeps",
        (shaped(2 * n + 5 * edge, LANES), shaped(5 * edge, LANES)),
        [VMEM] * 5,
        (VMEM, VMEM),
        10**6,
        500000,
    )(own, partner, near, far, inner)
    other = send(mine, layers)
    held, masks = lax.optimization_barrier((held, masks))
    base = call(
        grain_kernel, "grains", shaped(shells, nodes, LANES), [VMEM] * 2, VMEM, 10**9, 3000000
    )(held, grain_diffusion_matrix)
    next_warmth, warming, flux, grain, salt = call(
        functools.partial(reaction_kernel, sheets, blocks),
        "reaction",
        (
            shaped(n, LANES),
            shaped(n, LANES),
            shaped(n, LANES),
            shaped(shells, nodes, LANES),
            shaped(nodes, LANES),
        ),
        [VMEM] * 9,
        (HBM,) * 5,
        10**7,
        3000000,
        (
            pltpu.VMEM((2 * n, 2 * LANES), jnp.float32),
            pltpu.VMEM((n, 2 * LANES), jnp.float32),
            pltpu.VMEM((shells, nodes, LANES), jnp.float32),
            pltpu.SemaphoreType.DMA((4,)),
            pltpu.SemaphoreType.DMA((4,)),
        ),
    )(factors, mine, other, local, other_local, masks, base, link, turned)
    return (
        next_warmth.reshape(warmth_level.shape),
        warming.reshape(warmth_level.shape),
        flux.reshape(warmth_level.shape),
        grain.reshape(grain_shell_level.shape),
        salt.reshape(solution_salt_level.shape),
    )


def solution(mesh):
    placed = (
        P("layer", "tile", None),
        P("layer", "tile", None),
        P("layer", "tile", None),
        P(),
        P("layer", "tile", None),
        P("tile", None),
        P(),
        P(None, "tile", "layer"),
        P(None, None, "tile", "layer"),
        P(),
        P(),
    )
    tiles, parts = mesh.shape["tile"], mesh.shape["layer"]
    plan = functools.partial(per_device, tiles) if parts == 2 else per_device_general
    return jax.shard_map(
        plan,
        mesh=mesh,
        in_specs=placed,
        out_specs=(
            P("layer", "tile", None),
            P("layer", "tile", None),
            P("layer", "tile", None),
            P(None, None, "tile", "layer"),
            P(None, "tile", "layer"),
        ),
        check_vma=False,
    )
```

```python
import functools

import jax
import jax.numpy as jnp
from jax import lax
from jax.experimental import pallas as pl
from jax.experimental.pallas import tpu as pltpu
from jax.sharding import PartitionSpec as P

SWEEPS = 3
BV_ITERS = 4


warming_advance = 0.04
damping_weight = 4.5
imposed_excitation = 0.6
shell_flux = 0.5
film_resist = 0.5

LANES = 128
ROWS = 8
LOG2 = 0.6931471805599453
HIGHEST = lax.Precision.HIGHEST


def extended(block, sides, width):
    for axis, dim in sides:
        count = lax.axis_size(axis)
        forward = [(i, i + 1) for i in range(count - 1)]
        backward = [(target, source) for source, target in forward]
        low = lax.ppermute(
            lax.slice_in_dim(block, block.shape[dim] - width, None, axis=dim), axis, forward
        )
        high = lax.ppermute(lax.slice_in_dim(block, 0, width, axis=dim), axis, backward)
        block = jnp.concatenate([low, block, high], axis=dim)
    return block


def advance_stack_vertical(
    temp_col,
    volt_col,
    sheet_node_link_matrix,
    solution_salt_level,
    grain_shell_level,
    solution_diffusion_matrix,
    grain_diffusion_matrix,
):
    highest = lax.Precision.HIGHEST
    shells = grain_diffusion_matrix.shape[0]
    node_temp = jnp.einsum("el,lxy->exy", sheet_node_link_matrix, temp_col, precision=highest)
    node_voltage = jnp.einsum("el,lxy->exy", sheet_node_link_matrix, volt_col, precision=highest)
    next_solution_level = jnp.einsum(
        "ef,fxy->exy", solution_diffusion_matrix, solution_salt_level, precision=highest
    )
    surface_base = jnp.einsum(
        "s,sexy->exy", grain_diffusion_matrix[shells - 1], grain_shell_level, precision=highest
    )
    gain = shell_flux * grain_diffusion_matrix[shells - 1, shells - 1]
    rate = 0.5 * jax.nn.sigmoid(0.3 * node_temp) * jax.nn.sigmoid(next_solution_level)
    reaction = jnp.zeros_like(node_temp)
    for iteration in range(BV_ITERS):
        surface = surface_base - gain * reaction
        overvoltage = node_voltage - jnp.tanh(surface) - film_resist * reaction
        reaction = 2.0 * rate * jnp.sinh(0.5 * overvoltage)
    surface = surface_base - gain * reaction
    source = reaction * (node_voltage - jnp.tanh(surface))
    next_grain_level = jnp.einsum(
        "st,texy->sexy", grain_diffusion_matrix, grain_shell_level, precision=highest
    )
    next_grain_level = (
        next_grain_level
        - shell_flux * grain_diffusion_matrix[:, shells - 1][:, None, None, None] * reaction[None]
    )
    reaction_warming_sheets = jnp.einsum(
        "el,exy->lxy", sheet_node_link_matrix, source, precision=highest
    )
    reaction_flux_sheets = jnp.einsum(
        "el,exy->lxy", sheet_node_link_matrix, reaction, precision=highest
    )
    return (reaction_warming_sheets, reaction_flux_sheets, next_grain_level, next_solution_level)


def four_border_faces(bordered_lattice):
    return (
        bordered_lattice[:, 2:, 1:-1]
        + bordered_lattice[:, :-2, 1:-1]
        + bordered_lattice[:, 1:-1, 2:]
        + bordered_lattice[:, 1:-1, :-2]
    )


def per_device_general(
    warmth_level,
    heat_flow_ability,
    material_zone_label,
    reciprocal_warming_storage,
    collector_potential_field,
    tab_indicator,
    sheet_node_link_matrix,
    solution_salt_level,
    grain_shell_level,
    solution_diffusion_matrix,
    grain_diffusion_matrix,
):
    stored_coulomb_limit = jnp.zeros_like(warmth_level)
    for label in range(reciprocal_warming_storage.shape[0]):
        stored_coulomb_limit = stored_coulomb_limit + jnp.where(
            material_zone_label == label, reciprocal_warming_storage[label], 0.0
        )
    bordered_lattice = extended(warmth_level, (("tile", 1), ("layer", 0)), 1)
    bordered_lattice = jnp.pad(bordered_lattice, ((0, 0), (0, 0), (1, 1)))
    neighbour_entries = bordered_lattice[2:, 1:-1, 1:-1] + bordered_lattice[:-2, 1:-1, 1:-1]
    neighbour_entries = (
        neighbour_entries + bordered_lattice[1:-1, 2:, 1:-1] + bordered_lattice[1:-1, :-2, 1:-1]
    )
    neighbour_entries = (
        neighbour_entries + bordered_lattice[1:-1, 1:-1, 2:] + bordered_lattice[1:-1, 1:-1, :-2]
    )
    next_warmth_level = (
        warmth_level
        + warming_advance
        * stored_coulomb_limit
        * heat_flow_ability
        * (neighbour_entries - 6.0 * warmth_level)
    )
    bounded_entries = (1 - tab_indicator).astype(jnp.float32)[None]
    battery_potential_drop = collector_potential_field
    for sweep in range(SWEEPS):
        enclosed_lattice = extended(battery_potential_drop, (("tile", 1),), 1)
        enclosed_lattice = jnp.pad(enclosed_lattice, ((0, 0), (0, 0), (1, 1)))
        battery_potential_drop = (
            bounded_entries
            * (four_border_faces(enclosed_lattice) + imposed_excitation * next_warmth_level)
            / damping_weight
        )
    temp_col, volt_col = (
        lax.all_to_all(next_warmth_level, "layer", split_axis=2, concat_axis=0, tiled=True),
        lax.all_to_all(battery_potential_drop, "layer", split_axis=2, concat_axis=0, tiled=True),
    )
    heat_col, current_col, next_grain_level, next_solution_level = advance_stack_vertical(
        temp_col,
        volt_col,
        sheet_node_link_matrix,
        solution_salt_level,
        grain_shell_level,
        solution_diffusion_matrix,
        grain_diffusion_matrix,
    )
    reaction_warming_sheets, reaction_flux_sheets = (
        lax.all_to_all(heat_col, "layer", split_axis=0, concat_axis=2, tiled=True),
        lax.all_to_all(current_col, "layer", split_axis=0, concat_axis=2, tiled=True),
    )
    return (
        next_warmth_level,
        reaction_warming_sheets,
        reaction_flux_sheets,
        next_grain_level,
        next_solution_level,
    )


def along_span(field, blocks):
    rows = field.shape[0]
    lane = lax.broadcasted_iota(jnp.int32, field.shape, 1)
    block = lax.rem(lax.broadcasted_iota(jnp.int32, field.shape, 0), blocks)
    low = pltpu.roll(field, 1, 1)
    low_carry = jnp.where(block == 0, 0.0, pltpu.roll(low, 1, 0))
    high = pltpu.roll(field, LANES - 1, 1)
    high_carry = jnp.where(block == blocks - 1, 0.0, pltpu.roll(high, rows - 1, 0))
    return jnp.where(lane == 0, low_carry, low) + jnp.where(lane == LANES - 1, high_carry, high)


def along_sheets(field, blocks):
    rows = field.shape[0]
    row = lax.broadcasted_iota(jnp.int32, field.shape, 0)
    low = jnp.where(row < blocks, 0.0, pltpu.roll(field, blocks, 0))
    high = jnp.where(row >= rows - blocks, 0.0, pltpu.roll(field, rows - blocks, 0))
    return low + high


def fetch(pairs, sems):
    copies = [pltpu.make_async_copy(src, dst, sems.at[i]) for i, (src, dst) in enumerate(pairs)]
    for copy in copies:
        copy.start()
    return copies


def pack_kernel(
    blocks, storage, warmth, ability, zone, potential, tab, out, regions, heat, label, tabs, sems
):
    n = warmth.shape[0]
    copies = fetch(
        (
            (storage, regions),
            (zone, label),
            (ability, heat),
            (tab, tabs),
            (warmth, out.at[0:n]),
            (potential, out.at[n : 2 * n]),
        ),
        sems,
    )
    for copy in copies[:4]:
        copy.wait()
    zones = label[...]
    capacity = jnp.full(zones.shape, regions[0])
    for region in range(1, regions.shape[0]):
        capacity = jnp.where(zones == region, regions[region], capacity)
    out[2 * n : 3 * n, :] = warming_advance * capacity * heat[...]
    free = (1 - tabs[...]).astype(jnp.float32) * (1.0 / damping_weight)
    out[3 * n : 3 * n + blocks, :] = free
    out[3 * n + blocks : 3 * n + 2 * blocks, :] = free
    for copy in copies[4:]:
        copy.wait()


def spread(count, total, per):
    row = lax.broadcasted_iota(jnp.int32, (total, count), 0)
    column = lax.broadcasted_iota(jnp.int32, (total, count), 1)
    return (row // per == column).astype(jnp.float32)


def wide(matrix, per):
    rows, columns = matrix.shape
    left = spread(rows, rows * per, per)
    right = spread(columns, columns * per, per)
    full = jnp.dot(left, matrix, precision=HIGHEST, preferred_element_type=jnp.float32)
    full = lax.dot_general(
        full, right, (((1,), (1,)), ((), ())), precision=HIGHEST, preferred_element_type=jnp.float32
    )
    row = lax.broadcasted_iota(jnp.int32, full.shape, 0)
    column = lax.broadcasted_iota(jnp.int32, full.shape, 1)
    return jnp.where(lax.rem(row, per) == lax.rem(column, per), full, 0.0)


def halves(value):
    high = value.astype(jnp.bfloat16)
    return high, (value - high.astype(jnp.float32)).astype(jnp.bfloat16)


def link_kernel(blocks, parts, turned, wide_link, wide_turned):
    sheets, points = turned.shape
    per = blocks // parts
    own = sheets // parts
    rows, columns = points * blocks, sheets * blocks
    layer = lax.axis_index("layer")
    product = functools.partial(
        lax.dot_general, precision=HIGHEST, preferred_element_type=jnp.float32
    )
    plain, across = (((1,), (0,)), ((), ())), (((1,), (1,)), ((), ()))

    def iota(shape):
        return [lax.broadcasted_iota(jnp.int32, shape, axis) for axis in range(2)]

    def fits(r, c):
        part = lax.rem(r // (points * per) + layer, parts)
        return lax.rem(c, blocks) == part * per + lax.rem(r, per)

    r, c = iota((rows, points))
    pick = (lax.rem(r, points * per) // per == c).astype(jnp.float32)
    r, c = iota((sheets, columns))
    split = (c // blocks == r).astype(jnp.float32)
    full = product(product(pick, turned[...], across), split, plain)
    r, c = iota((rows, columns))
    wide_link[...] = jnp.where(fits(r, c), full, 0.0)
    r, c = iota((own * blocks, sheets))
    split = (r // blocks + own * layer == c).astype(jnp.float32)
    full = product(product(split, turned[...], plain), pick, across)
    r, c = iota((own * blocks, rows))
    wide_turned[...] = jnp.where(fits(c, r), full, 0.0)


def local_kernel(
    diffusion,
    grain,
    salt,
    salt_matrix,
    held,
    local,
    factors,
    weights,
    level,
    matrix,
    sems,
    grain_sems,
):
    shells, nodes, _ = grain.shape
    part = shells // grain_sems.shape[0]
    small = fetch(((salt, level), (salt_matrix, matrix), (diffusion, weights)), sems)
    copies = fetch(
        [(grain.at[s : s + part], held.at[s : s + part]) for s in range(0, shells, part)],
        grain_sems,
    )
    for copy in small:
        copy.wait()
    points = matrix.shape[0]
    per = nodes // points
    spans = [level[pl.ds(i, points, stride=per), :] for i in range(per)]
    spans = jnp.dot(
        matrix[...],
        jnp.concatenate(spans, axis=1),
        precision=HIGHEST,
        preferred_element_type=jnp.float32,
    )
    for i in range(per):
        local[pl.ds(nodes + i, points, stride=per), :] = spans[:, i * LANES : (i + 1) * LANES]
    for shell in range(shells):
        factors[shell : shell + 1, :] = jnp.full(
            (1, LANES), shell_flux * weights[shell, shells - 1]
        )
    surface = jnp.zeros((nodes, LANES), jnp.float32)
    for i, copy in enumerate(copies):
        copy.wait()
        for shell in range(i * part, (i + 1) * part):
            surface = surface + weights[shells - 1, shell] * held[shell]
    local[0:nodes, :] = surface


def grain_kernel(grain, weights, base):
    shells, count, _ = grain.shape
    matrix_high, matrix_low = halves(wide(weights[...], ROWS))
    for start in range(0, count, 2 * ROWS):
        pair = [
            grain[:, start + k * ROWS : start + (k + 1) * ROWS, :].reshape(shells * ROWS, LANES)
            for k in range(2)
        ]
        high, low = halves(jnp.concatenate(pair, axis=1))
        dot = functools.partial(jnp.dot, preferred_element_type=jnp.float32)
        result = dot(matrix_high, high) + (dot(matrix_high, low) + dot(matrix_low, high))
        for k in range(2):
            part = result[:, k * LANES : (k + 1) * LANES].reshape(shells, ROWS, LANES)
            base[:, start + k * ROWS : start + (k + 1) * ROWS, :] = part


def sweep_kernel(sheets, blocks, tiles, own, partner, near, far, inner, out, masks):
    n = sheets * blocks
    size = own.shape[0]
    tile = lax.axis_index("tile")
    block = lax.axis_index("layer")
    first = jnp.logical_or(tile == 0, tile == tiles - 1)
    second = jnp.logical_or(tile == 2, tile == tiles - 3)
    beside = jnp.logical_or(tile == 1, tile == tiles - 2)
    keep_outer = jnp.where(first, 0.0, 1.0)
    keep_far = jnp.where(jnp.logical_or(first, second), 0.0, 1.0)
    keep_inner = jnp.where(beside, 0.0, 1.0)

    def load(ref, start, rows, keep=None):
        value = ref[start : start + rows, :]
        return value if keep is None else keep * value

    def window(start, rows):
        return [
            load(near, size + start, rows, keep_outer),
            load(near, start, rows, keep_outer),
            load(own, start, rows),
            load(partner, start, rows),
            load(inner, start, rows, keep_inner),
        ]

    warmth = [load(far, 0, n, keep_far)] + window(0, n) + [load(inner, size, n, keep_inner)]
    volt = [load(far, n, n, keep_far)] + window(n, n) + [load(inner, size + n, n, keep_inner)]
    slope = window(2 * n, n)
    free = window(3 * n, 2 * blocks)
    for i in range(5):
        masks[2 * i * blocks : 2 * (i + 1) * blocks, :] = free[i]
    free = [jnp.concatenate([m] * (n // m.shape[0]), axis=0) for m in free]
    temp = []
    for i in range(5):
        w = warmth[i + 1]
        around = warmth[i] + warmth[i + 2] + along_sheets(w, blocks) + along_span(w, blocks)
        temp.append(w + slope[i] * (around - 6.0 * w))
    for sweep in range(SWEEPS):
        volt = [
            free[i + sweep]
            * (
                volt[i]
                + volt[i + 2]
                + along_span(volt[i + 1], blocks)
                + imposed_excitation * temp[i + sweep]
            )
            for i in range(len(volt) - 2)
        ]
    out[0:n, :] = temp[2]
    out[n : 2 * n, :] = volt[0]
    for i in range(5):
        for k, value in enumerate((warmth[i + 1], slope[i])):
            edge = jnp.where(block == 0, value[n - blocks :, :], value[0:blocks, :])
            start = 2 * n + (2 * i + k) * blocks
            out[start : start + blocks, :] = edge


def react(surface_base, gain, rate, node_voltage):
    reaction = jnp.zeros_like(node_voltage)
    for iteration in range(BV_ITERS):
        surface = surface_base - gain * reaction
        half = 0.5 * (node_voltage - jnp.tanh(surface) - film_resist * reaction)
        reaction = rate * (jnp.exp(half - LOG2) - jnp.exp(-half - LOG2))
    surface = surface_base - gain * reaction
    return reaction, reaction * (node_voltage - jnp.tanh(surface))


def reaction_kernel(
    sheets,
    blocks,
    factors,
    mine,
    other,
    local,
    other_local,
    masks,
    base,
    link,
    turned,
    next_warmth,
    warming,
    flux,
    grain_out,
    salt_out,
    both,
    sheets_now,
    copy_out,
    sems,
    grain_sems,
):
    n = sheets * blocks
    shells, nodes, _ = base.shape
    block = lax.axis_index("layer")
    edge = 2 * blocks
    early = fetch(((local.at[nodes : 2 * nodes], salt_out),), sems)

    free = [masks[i * edge : (i + 1) * edge, :] for i in range(5)]
    added = []
    for i in range(5):
        at = 2 * n + i * edge
        added.append(pltpu.roll(mine[at : at + edge, :], blocks, 0) * other[at : at + edge, :])
    volt = [jnp.zeros_like(added[0])] * 7
    for sweep in range(SWEEPS):
        volt = [
            free[i + sweep]
            * (
                volt[i]
                + volt[i + 2]
                + along_span(volt[i + 1], blocks)
                + imposed_excitation * added[i + sweep]
            )
            for i in range(len(volt) - 2)
        ]
    here = pl.ds(pl.multiple_of(block * n, ROWS), n)
    there = pl.ds(pl.multiple_of((1 - block) * n, ROWS), n)
    both[here, 0:LANES] = mine[0:n, :]
    both[there, 0:LANES] = other[0:n, :]
    both[here, LANES:] = mine[n : 2 * n, :]
    both[there, LANES:] = other[n : 2 * n, :]
    extra = jnp.concatenate([added[2], volt[0]], axis=1)
    extra = jnp.where(block == 0, extra, pltpu.roll(extra, blocks, 0))
    both[n - blocks : n + blocks, :] += extra
    warmth_copy = pltpu.make_async_copy(both.at[here, 0:LANES], next_warmth, sems.at[1])
    warmth_copy.start()

    dot = functools.partial(jnp.dot, precision=HIGHEST, preferred_element_type=jnp.float32)
    node = dot(link[...], both[...])
    gain = factors[shells - 1 :, :]
    surface_base = jnp.concatenate([local[0:nodes, :], other_local[0:nodes, :]], axis=0)
    salt = jnp.concatenate(
        [local[nodes : 2 * nodes, :], other_local[nodes : 2 * nodes, :]], axis=0
    )
    rate = 1.0 / ((1.0 + jnp.exp(-0.3 * node[:, 0:LANES])) * (1.0 + jnp.exp(-salt)))
    reaction, source = react(surface_base, gain, rate, node[:, LANES:])
    sheets_now[...] = dot(turned[...], jnp.concatenate([source, reaction], axis=1))
    late = [
        pltpu.make_async_copy(sheets_now.at[:, 0:LANES], warming, sems.at[2]),
        pltpu.make_async_copy(sheets_now.at[:, LANES:], flux, sems.at[3]),
    ]
    for copy in late:
        copy.start()
    copies = []
    step = shells // grain_sems.shape[0]
    for first in range(0, shells, step):
        for shell in range(first, first + step):
            factor = factors[shell : shell + 1, :]
            copy_out[shell] = base[shell] - factor * reaction[0:nodes, :]
        copies.append(
            pltpu.make_async_copy(
                copy_out.at[first : first + step],
                grain_out.at[first : first + step],
                grain_sems.at[first // step],
            )
        )
        copies[-1].start()
    for copy in early + [warmth_copy] + copies + late:
        copy.wait()


VMEM = pl.BlockSpec(memory_space=pltpu.VMEM)
SMEM = pl.BlockSpec(memory_space=pltpu.SMEM)
HBM = pl.BlockSpec(memory_space=pltpu.HBM)


def in_hbm(*values):
    return [pltpu.with_memory_space_constraint(value, pltpu.HBM) for value in values]


def shaped(*shape):
    return jax.ShapeDtypeStruct(shape, jnp.float32)


def call(kernel, name, out, ins, outs, flops, nbytes, scratch=()):
    return pl.pallas_call(
        kernel,
        out_shape=out,
        in_specs=ins,
        out_specs=outs,
        scratch_shapes=scratch,
        compiler_params=pltpu.CompilerParams(vmem_limit_bytes=32 * 1024 * 1024),
        cost_estimate=pl.CostEstimate(flops=flops, bytes_accessed=nbytes, transcendentals=0),
        name=name,
    )


def per_device(
    tiles,
    warmth_level,
    heat_flow_ability,
    material_zone_label,
    reciprocal_warming_storage,
    collector_potential_field,
    tab_indicator,
    sheet_node_link_matrix,
    solution_salt_level,
    grain_shell_level,
    solution_diffusion_matrix,
    grain_diffusion_matrix,
):
    sheets, _, span = warmth_level.shape
    shells, points, _, part = grain_shell_level.shape
    blocks = span // LANES
    nodes = points * part // LANES
    n = sheets * blocks
    edge = 2 * blocks
    size = 3 * n + edge

    def both_layers(pairs):
        return [(s * 2 + j, t * 2 + j) for s, t in pairs for j in range(2)]

    def across(where):
        return [(t * 2 + j, t * 2 + 1 - j) for t in where for j in range(2)]

    def mutual(pairs):
        return pairs + [(t, s) for s, t in pairs]

    def send(value, pairs):
        return lax.ppermute(value, ("tile", "layer"), pairs)

    cores = both_layers(mutual([(t, t + 1) for t in range(0, tiles, 2)]))
    beside = both_layers(mutual([(t, t - 1) for t in range(2, tiles, 2)]))
    beside = beside + across([0, tiles - 1])
    beyond = both_layers(mutual([(t, t - 3) for t in range(4, tiles, 2)]))
    beyond = beyond + across([0, 2, tiles - 3, tiles - 1])
    layers = across(range(tiles))

    own = call(
        functools.partial(pack_kernel, blocks),
        "pack",
        shaped(3 * n + edge, LANES),
        [HBM] * 6,
        VMEM,
        1000,
        100000,
        (
            pltpu.SMEM(reciprocal_warming_storage.shape, jnp.float32),
            pltpu.VMEM((n, LANES), jnp.float32),
            pltpu.VMEM((n, LANES), jnp.int32),
            pltpu.VMEM((blocks, LANES), jnp.int32),
            pltpu.SemaphoreType.DMA((6,)),
        ),
    )(
        *in_hbm(
            reciprocal_warming_storage,
            warmth_level.reshape(n, LANES),
            heat_flow_ability.reshape(n, LANES),
            material_zone_label.reshape(n, LANES),
            collector_potential_field.reshape(n, LANES),
            tab_indicator.reshape(blocks, LANES),
        )
    )
    partner = send(own, cores)
    near = send(jnp.concatenate([own, partner], axis=0), beside)
    far = send(own[0 : 2 * n], beyond)
    held, local, factors = call(
        local_kernel,
        "columns",
        (
            shaped(shells, nodes, LANES),
            shaped(2 * nodes + 2 * ROWS, LANES),
            shaped(shells, LANES),
        ),
        [HBM] * 4,
        (VMEM,) * 3,
        10**7,
        3000000,
        (
            pltpu.SMEM(grain_diffusion_matrix.shape, jnp.float32),
            pltpu.VMEM((nodes, LANES), jnp.float32),
            pltpu.VMEM(solution_diffusion_matrix.shape, jnp.float32),
            pltpu.SemaphoreType.DMA((3,)),
            pltpu.SemaphoreType.DMA((4,)),
        ),
    )(
        *in_hbm(
            grain_diffusion_matrix,
            grain_shell_level.reshape(shells, nodes, LANES),
            solution_salt_level.reshape(nodes, LANES),
            solution_diffusion_matrix,
        )
    )
    other_local = send(local, layers)
    near, far, held, local, turned = lax.optimization_barrier(
        (near, far, held, local, sheet_node_link_matrix.T)
    )
    link, turned = call(
        functools.partial(link_kernel, blocks, 2),
        "links",
        (shaped(points * blocks, 2 * n), shaped(n, points * blocks)),
        [VMEM],
        (VMEM, VMEM),
        10**6,
        100000,
    )(turned)
    inner = send(near[0 : size + 2 * n], cores)
    mine, masks = call(
        functools.partial(sweep_kernel, sheets, blocks, tiles),
        "sweeps",
        (shaped(2 * n + 5 * edge, LANES), shaped(5 * edge, LANES)),
        [VMEM] * 5,
        (VMEM, VMEM),
        10**6,
        500000,
    )(own, partner, near, far, inner)
    other = send(mine, layers)
    held, masks, other_local = lax.optimization_barrier((held, masks, other_local))
    base = call(
        grain_kernel, "grains", shaped(shells, nodes, LANES), [VMEM] * 2, VMEM, 10**9, 3000000
    )(held, grain_diffusion_matrix)
    next_warmth, warming, flux, grain, salt = call(
        functools.partial(reaction_kernel, sheets, blocks),
        "reaction",
        (
            shaped(n, LANES),
            shaped(n, LANES),
            shaped(n, LANES),
            shaped(shells, nodes, LANES),
            shaped(nodes, LANES),
        ),
        [VMEM] * 9,
        (HBM,) * 5,
        10**7,
        3000000,
        (
            pltpu.VMEM((2 * n, 2 * LANES), jnp.float32),
            pltpu.VMEM((n, 2 * LANES), jnp.float32),
            pltpu.VMEM((shells, nodes, LANES), jnp.float32),
            pltpu.SemaphoreType.DMA((4,)),
            pltpu.SemaphoreType.DMA((4,)),
        ),
    )(factors, mine, other, local, other_local, masks, base, link, turned)
    return (
        next_warmth.reshape(warmth_level.shape),
        warming.reshape(warmth_level.shape),
        flux.reshape(warmth_level.shape),
        grain.reshape(grain_shell_level.shape),
        salt.reshape(solution_salt_level.shape),
    )


def solution(mesh):
    placed = (
        P("layer", "tile", None),
        P("layer", "tile", None),
        P("layer", "tile", None),
        P(),
        P("layer", "tile", None),
        P("tile", None),
        P(),
        P(None, "tile", "layer"),
        P(None, None, "tile", "layer"),
        P(),
        P(),
    )
    tiles, parts = mesh.shape["tile"], mesh.shape["layer"]
    plan = functools.partial(per_device, tiles) if parts == 2 else per_device_general
    return jax.shard_map(
        plan,
        mesh=mesh,
        in_specs=placed,
        out_specs=(
            P("layer", "tile", None),
            P("layer", "tile", None),
            P("layer", "tile", None),
            P(None, None, "tile", "layer"),
            P(None, "tile", "layer"),
        ),
        check_vma=False,
    )
```

```python
import functools

import jax
import jax.numpy as jnp
from jax import lax
from jax.experimental import pallas as pl
from jax.experimental.pallas import tpu as pltpu
from jax.sharding import PartitionSpec as P

SWEEPS = 3
BV_ITERS = 4


warming_advance = 0.04
damping_weight = 4.5
imposed_excitation = 0.6
shell_flux = 0.5
film_resist = 0.5

LANES = 128
ROWS = 8
LOG2 = 0.6931471805599453
HIGHEST = lax.Precision.HIGHEST


def extended(block, sides, width):
    for axis, dim in sides:
        count = lax.axis_size(axis)
        forward = [(i, i + 1) for i in range(count - 1)]
        backward = [(target, source) for source, target in forward]
        low = lax.ppermute(
            lax.slice_in_dim(block, block.shape[dim] - width, None, axis=dim), axis, forward
        )
        high = lax.ppermute(lax.slice_in_dim(block, 0, width, axis=dim), axis, backward)
        block = jnp.concatenate([low, block, high], axis=dim)
    return block


def advance_stack_vertical(
    temp_col,
    volt_col,
    sheet_node_link_matrix,
    solution_salt_level,
    grain_shell_level,
    solution_diffusion_matrix,
    grain_diffusion_matrix,
):
    highest = lax.Precision.HIGHEST
    shells = grain_diffusion_matrix.shape[0]
    node_temp = jnp.einsum("el,lxy->exy", sheet_node_link_matrix, temp_col, precision=highest)
    node_voltage = jnp.einsum("el,lxy->exy", sheet_node_link_matrix, volt_col, precision=highest)
    next_solution_level = jnp.einsum(
        "ef,fxy->exy", solution_diffusion_matrix, solution_salt_level, precision=highest
    )
    surface_base = jnp.einsum(
        "s,sexy->exy", grain_diffusion_matrix[shells - 1], grain_shell_level, precision=highest
    )
    gain = shell_flux * grain_diffusion_matrix[shells - 1, shells - 1]
    rate = 0.5 * jax.nn.sigmoid(0.3 * node_temp) * jax.nn.sigmoid(next_solution_level)
    reaction = jnp.zeros_like(node_temp)
    for iteration in range(BV_ITERS):
        surface = surface_base - gain * reaction
        overvoltage = node_voltage - jnp.tanh(surface) - film_resist * reaction
        reaction = 2.0 * rate * jnp.sinh(0.5 * overvoltage)
    surface = surface_base - gain * reaction
    source = reaction * (node_voltage - jnp.tanh(surface))
    next_grain_level = jnp.einsum(
        "st,texy->sexy", grain_diffusion_matrix, grain_shell_level, precision=highest
    )
    next_grain_level = (
        next_grain_level
        - shell_flux * grain_diffusion_matrix[:, shells - 1][:, None, None, None] * reaction[None]
    )
    reaction_warming_sheets = jnp.einsum(
        "el,exy->lxy", sheet_node_link_matrix, source, precision=highest
    )
    reaction_flux_sheets = jnp.einsum(
        "el,exy->lxy", sheet_node_link_matrix, reaction, precision=highest
    )
    return (reaction_warming_sheets, reaction_flux_sheets, next_grain_level, next_solution_level)


def four_border_faces(bordered_lattice):
    return (
        bordered_lattice[:, 2:, 1:-1]
        + bordered_lattice[:, :-2, 1:-1]
        + bordered_lattice[:, 1:-1, 2:]
        + bordered_lattice[:, 1:-1, :-2]
    )


def per_device_general(
    warmth_level,
    heat_flow_ability,
    material_zone_label,
    reciprocal_warming_storage,
    collector_potential_field,
    tab_indicator,
    sheet_node_link_matrix,
    solution_salt_level,
    grain_shell_level,
    solution_diffusion_matrix,
    grain_diffusion_matrix,
):
    stored_coulomb_limit = jnp.zeros_like(warmth_level)
    for label in range(reciprocal_warming_storage.shape[0]):
        stored_coulomb_limit = stored_coulomb_limit + jnp.where(
            material_zone_label == label, reciprocal_warming_storage[label], 0.0
        )
    bordered_lattice = extended(warmth_level, (("tile", 1), ("layer", 0)), 1)
    bordered_lattice = jnp.pad(bordered_lattice, ((0, 0), (0, 0), (1, 1)))
    neighbour_entries = bordered_lattice[2:, 1:-1, 1:-1] + bordered_lattice[:-2, 1:-1, 1:-1]
    neighbour_entries = (
        neighbour_entries + bordered_lattice[1:-1, 2:, 1:-1] + bordered_lattice[1:-1, :-2, 1:-1]
    )
    neighbour_entries = (
        neighbour_entries + bordered_lattice[1:-1, 1:-1, 2:] + bordered_lattice[1:-1, 1:-1, :-2]
    )
    next_warmth_level = (
        warmth_level
        + warming_advance
        * stored_coulomb_limit
        * heat_flow_ability
        * (neighbour_entries - 6.0 * warmth_level)
    )
    bounded_entries = (1 - tab_indicator).astype(jnp.float32)[None]
    battery_potential_drop = collector_potential_field
    for sweep in range(SWEEPS):
        enclosed_lattice = extended(battery_potential_drop, (("tile", 1),), 1)
        enclosed_lattice = jnp.pad(enclosed_lattice, ((0, 0), (0, 0), (1, 1)))
        battery_potential_drop = (
            bounded_entries
            * (four_border_faces(enclosed_lattice) + imposed_excitation * next_warmth_level)
            / damping_weight
        )
    temp_col, volt_col = (
        lax.all_to_all(next_warmth_level, "layer", split_axis=2, concat_axis=0, tiled=True),
        lax.all_to_all(battery_potential_drop, "layer", split_axis=2, concat_axis=0, tiled=True),
    )
    heat_col, current_col, next_grain_level, next_solution_level = advance_stack_vertical(
        temp_col,
        volt_col,
        sheet_node_link_matrix,
        solution_salt_level,
        grain_shell_level,
        solution_diffusion_matrix,
        grain_diffusion_matrix,
    )
    reaction_warming_sheets, reaction_flux_sheets = (
        lax.all_to_all(heat_col, "layer", split_axis=0, concat_axis=2, tiled=True),
        lax.all_to_all(current_col, "layer", split_axis=0, concat_axis=2, tiled=True),
    )
    return (
        next_warmth_level,
        reaction_warming_sheets,
        reaction_flux_sheets,
        next_grain_level,
        next_solution_level,
    )


def along_span(field, blocks):
    rows = field.shape[0]
    lane = lax.broadcasted_iota(jnp.int32, field.shape, 1)
    block = lax.rem(lax.broadcasted_iota(jnp.int32, field.shape, 0), blocks)
    low = pltpu.roll(field, 1, 1)
    low_carry = jnp.where(block == 0, 0.0, pltpu.roll(low, 1, 0))
    high = pltpu.roll(field, LANES - 1, 1)
    high_carry = jnp.where(block == blocks - 1, 0.0, pltpu.roll(high, rows - 1, 0))
    return jnp.where(lane == 0, low_carry, low) + jnp.where(lane == LANES - 1, high_carry, high)


def along_sheets(field, blocks):
    rows = field.shape[0]
    row = lax.broadcasted_iota(jnp.int32, field.shape, 0)
    low = jnp.where(row < blocks, 0.0, pltpu.roll(field, blocks, 0))
    high = jnp.where(row >= rows - blocks, 0.0, pltpu.roll(field, rows - blocks, 0))
    return low + high


def fetch(pairs, sems):
    copies = [pltpu.make_async_copy(src, dst, sems.at[i]) for i, (src, dst) in enumerate(pairs)]
    for copy in copies:
        copy.start()
    return copies


def pack_kernel(
    blocks, storage, warmth, ability, zone, potential, tab, out, regions, heat, label, tabs, sems
):
    n = warmth.shape[0]
    copies = fetch(
        (
            (storage, regions),
            (zone, label),
            (ability, heat),
            (tab, tabs),
            (warmth, out.at[0:n]),
            (potential, out.at[n : 2 * n]),
        ),
        sems,
    )
    for copy in copies[:4]:
        copy.wait()
    zones = label[...]
    capacity = jnp.full(zones.shape, regions[0])
    for region in range(1, regions.shape[0]):
        capacity = jnp.where(zones == region, regions[region], capacity)
    out[2 * n : 3 * n, :] = warming_advance * capacity * heat[...]
    free = (1 - tabs[...]).astype(jnp.float32) * (1.0 / damping_weight)
    out[3 * n : 3 * n + blocks, :] = free
    out[3 * n + blocks : 3 * n + 2 * blocks, :] = free
    for copy in copies[4:]:
        copy.wait()


def spread(count, total, per):
    row = lax.broadcasted_iota(jnp.int32, (total, count), 0)
    column = lax.broadcasted_iota(jnp.int32, (total, count), 1)
    return (row // per == column).astype(jnp.float32)


def wide(matrix, per):
    rows, columns = matrix.shape
    left = spread(rows, rows * per, per)
    right = spread(columns, columns * per, per)
    full = jnp.dot(left, matrix, precision=HIGHEST, preferred_element_type=jnp.float32)
    full = lax.dot_general(
        full, right, (((1,), (1,)), ((), ())), precision=HIGHEST, preferred_element_type=jnp.float32
    )
    row = lax.broadcasted_iota(jnp.int32, full.shape, 0)
    column = lax.broadcasted_iota(jnp.int32, full.shape, 1)
    return jnp.where(lax.rem(row, per) == lax.rem(column, per), full, 0.0)


def halves(value):
    high = value.astype(jnp.bfloat16)
    return high, (value - high.astype(jnp.float32)).astype(jnp.bfloat16)


def link_kernel(blocks, parts, turned, wide_link, wide_turned):
    sheets, points = turned.shape
    per = blocks // parts
    own = sheets // parts
    rows, columns = points * blocks, sheets * blocks
    layer = lax.axis_index("layer")
    product = functools.partial(
        lax.dot_general, precision=HIGHEST, preferred_element_type=jnp.float32
    )
    plain, across = (((1,), (0,)), ((), ())), (((1,), (1,)), ((), ()))

    def iota(shape):
        return [lax.broadcasted_iota(jnp.int32, shape, axis) for axis in range(2)]

    def fits(r, c):
        part = lax.rem(r // (points * per) + layer, parts)
        return lax.rem(c, blocks) == part * per + lax.rem(r, per)

    r, c = iota((rows, points))
    pick = (lax.rem(r, points * per) // per == c).astype(jnp.float32)
    r, c = iota((sheets, columns))
    split = (c // blocks == r).astype(jnp.float32)
    full = product(product(pick, turned[...], across), split, plain)
    r, c = iota((rows, columns))
    wide_link[...] = jnp.where(fits(r, c), full, 0.0)
    r, c = iota((own * blocks, sheets))
    split = (r // blocks + own * layer == c).astype(jnp.float32)
    full = product(product(split, turned[...], plain), pick, across)
    r, c = iota((own * blocks, rows))
    wide_turned[...] = jnp.where(fits(c, r), full, 0.0)


def local_kernel(
    diffusion,
    grain,
    salt,
    salt_matrix,
    held,
    local,
    factors,
    weights,
    level,
    matrix,
    sems,
    grain_sems,
):
    shells, nodes, _ = grain.shape
    part = shells // grain_sems.shape[0]
    small = fetch(((salt, level), (salt_matrix, matrix), (diffusion, weights)), sems)
    copies = fetch(
        [(grain.at[s : s + part], held.at[s : s + part]) for s in range(0, shells, part)],
        grain_sems,
    )
    for copy in small:
        copy.wait()
    points = matrix.shape[0]
    per = nodes // points
    spans = [level[pl.ds(i, points, stride=per), :] for i in range(per)]
    spans = jnp.dot(
        matrix[...],
        jnp.concatenate(spans, axis=1),
        precision=HIGHEST,
        preferred_element_type=jnp.float32,
    )
    for i in range(per):
        local[pl.ds(nodes + i, points, stride=per), :] = spans[:, i * LANES : (i + 1) * LANES]
    for shell in range(shells):
        factors[shell : shell + 1, :] = jnp.full(
            (1, LANES), shell_flux * weights[shell, shells - 1]
        )
    surface = jnp.zeros((nodes, LANES), jnp.float32)
    for i, copy in enumerate(copies):
        copy.wait()
        for shell in range(i * part, (i + 1) * part):
            surface = surface + weights[shells - 1, shell] * held[shell]
    local[0:nodes, :] = surface


def grain_kernel(grain, weights, base):
    shells, count, _ = grain.shape
    matrix_high, matrix_low = halves(wide(weights[...], ROWS))
    for start in range(0, count, 2 * ROWS):
        pair = [
            grain[:, start + k * ROWS : start + (k + 1) * ROWS, :].reshape(shells * ROWS, LANES)
            for k in range(2)
        ]
        high, low = halves(jnp.concatenate(pair, axis=1))
        dot = functools.partial(jnp.dot, preferred_element_type=jnp.float32)
        result = dot(matrix_high, high) + (dot(matrix_high, low) + dot(matrix_low, high))
        for k in range(2):
            part = result[:, k * LANES : (k + 1) * LANES].reshape(shells, ROWS, LANES)
            base[:, start + k * ROWS : start + (k + 1) * ROWS, :] = part


def sweep_kernel(
    sheets, blocks, tiles, own, partner, near, skip, far, near_in, skip_in, out, masks
):
    n = sheets * blocks
    tile = lax.axis_index("tile")
    block = lax.axis_index("layer")
    first = jnp.logical_or(tile == 0, tile == tiles - 1)
    second = jnp.logical_or(tile == 2, tile == tiles - 3)
    beside = jnp.logical_or(tile == 1, tile == tiles - 2)
    keep_outer = jnp.where(first, 0.0, 1.0)
    keep_far = jnp.where(jnp.logical_or(first, second), 0.0, 1.0)
    keep_inner = jnp.where(beside, 0.0, 1.0)

    def load(ref, start, rows, keep=None):
        value = ref[start : start + rows, :]
        return value if keep is None else keep * value

    def window(start, rows):
        return [
            load(skip_in, start, rows, keep_outer),
            load(near, start, rows, keep_outer),
            load(own, start, rows),
            load(partner, start, rows),
            load(near_in, start, rows, keep_inner),
        ]

    warmth = [load(far, 0, n, keep_far)] + window(0, n) + [load(skip, 0, n, keep_inner)]
    volt = [load(far, n, n, keep_far)] + window(n, n) + [load(skip, n, n, keep_inner)]
    slope = window(2 * n, n)
    free = window(3 * n, 2 * blocks)
    for i in range(5):
        masks[2 * i * blocks : 2 * (i + 1) * blocks, :] = free[i]
    free = [jnp.concatenate([m] * (n // m.shape[0]), axis=0) for m in free]
    temp = []
    for i in range(5):
        w = warmth[i + 1]
        around = warmth[i] + warmth[i + 2] + along_sheets(w, blocks) + along_span(w, blocks)
        temp.append(w + slope[i] * (around - 6.0 * w))
    for sweep in range(SWEEPS):
        volt = [
            free[i + sweep]
            * (
                volt[i]
                + volt[i + 2]
                + along_span(volt[i + 1], blocks)
                + imposed_excitation * temp[i + sweep]
            )
            for i in range(len(volt) - 2)
        ]
    out[0:n, :] = temp[2]
    out[n : 2 * n, :] = volt[0]
    for i in range(5):
        for k, value in enumerate((warmth[i + 1], slope[i])):
            edge = jnp.where(block == 0, value[n - blocks :, :], value[0:blocks, :])
            start = 2 * n + (2 * i + k) * blocks
            out[start : start + blocks, :] = edge


def react(surface_base, gain, rate, node_voltage):
    reaction = jnp.zeros_like(node_voltage)
    for iteration in range(BV_ITERS):
        surface = surface_base - gain * reaction
        half = 0.5 * (node_voltage - jnp.tanh(surface) - film_resist * reaction)
        reaction = rate * (jnp.exp(half - LOG2) - jnp.exp(-half - LOG2))
    surface = surface_base - gain * reaction
    return reaction, reaction * (node_voltage - jnp.tanh(surface))


def reaction_kernel(
    sheets,
    blocks,
    factors,
    mine,
    other,
    local,
    other_local,
    masks,
    base,
    link,
    turned,
    next_warmth,
    warming,
    flux,
    grain_out,
    salt_out,
    both,
    sheets_now,
    copy_out,
    sems,
    grain_sems,
):
    n = sheets * blocks
    shells, nodes, _ = base.shape
    block = lax.axis_index("layer")
    edge = 2 * blocks
    early = fetch(((local.at[nodes : 2 * nodes], salt_out),), sems)

    free = [masks[i * edge : (i + 1) * edge, :] for i in range(5)]
    added = []
    for i in range(5):
        at = 2 * n + i * edge
        added.append(pltpu.roll(mine[at : at + edge, :], blocks, 0) * other[at : at + edge, :])
    volt = [jnp.zeros_like(added[0])] * 7
    for sweep in range(SWEEPS):
        volt = [
            free[i + sweep]
            * (
                volt[i]
                + volt[i + 2]
                + along_span(volt[i + 1], blocks)
                + imposed_excitation * added[i + sweep]
            )
            for i in range(len(volt) - 2)
        ]
    here = pl.ds(pl.multiple_of(block * n, ROWS), n)
    there = pl.ds(pl.multiple_of((1 - block) * n, ROWS), n)
    both[here, 0:LANES] = mine[0:n, :]
    both[there, 0:LANES] = other[0:n, :]
    both[here, LANES:] = mine[n : 2 * n, :]
    both[there, LANES:] = other[n : 2 * n, :]
    extra = jnp.concatenate([added[2], volt[0]], axis=1)
    extra = jnp.where(block == 0, extra, pltpu.roll(extra, blocks, 0))
    both[n - blocks : n + blocks, :] += extra
    warmth_copy = pltpu.make_async_copy(both.at[here, 0:LANES], next_warmth, sems.at[1])
    warmth_copy.start()

    dot = functools.partial(jnp.dot, precision=HIGHEST, preferred_element_type=jnp.float32)
    node = dot(link[...], both[...])
    gain = factors[shells - 1 :, :]
    surface_base = jnp.concatenate([local[0:nodes, :], other_local[0:nodes, :]], axis=0)
    salt = jnp.concatenate(
        [local[nodes : 2 * nodes, :], other_local[nodes : 2 * nodes, :]], axis=0
    )
    rate = 1.0 / ((1.0 + jnp.exp(-0.3 * node[:, 0:LANES])) * (1.0 + jnp.exp(-salt)))
    reaction, source = react(surface_base, gain, rate, node[:, LANES:])
    sheets_now[...] = dot(turned[...], jnp.concatenate([source, reaction], axis=1))
    late = [
        pltpu.make_async_copy(sheets_now.at[:, 0:LANES], warming, sems.at[2]),
        pltpu.make_async_copy(sheets_now.at[:, LANES:], flux, sems.at[3]),
    ]
    for copy in late:
        copy.start()
    copies = []
    step = shells // grain_sems.shape[0]
    for first in range(0, shells, step):
        for shell in range(first, first + step):
            factor = factors[shell : shell + 1, :]
            copy_out[shell] = base[shell] - factor * reaction[0:nodes, :]
        copies.append(
            pltpu.make_async_copy(
                copy_out.at[first : first + step],
                grain_out.at[first : first + step],
                grain_sems.at[first // step],
            )
        )
        copies[-1].start()
    for copy in early + [warmth_copy] + copies + late:
        copy.wait()


VMEM = pl.BlockSpec(memory_space=pltpu.VMEM)
SMEM = pl.BlockSpec(memory_space=pltpu.SMEM)
HBM = pl.BlockSpec(memory_space=pltpu.HBM)


def in_hbm(*values):
    return [pltpu.with_memory_space_constraint(value, pltpu.HBM) for value in values]


def shaped(*shape):
    return jax.ShapeDtypeStruct(shape, jnp.float32)


def call(kernel, name, out, ins, outs, flops, nbytes, scratch=()):
    return pl.pallas_call(
        kernel,
        out_shape=out,
        in_specs=ins,
        out_specs=outs,
        scratch_shapes=scratch,
        compiler_params=pltpu.CompilerParams(vmem_limit_bytes=32 * 1024 * 1024),
        cost_estimate=pl.CostEstimate(flops=flops, bytes_accessed=nbytes, transcendentals=0),
        name=name,
    )


def per_device(
    tiles,
    warmth_level,
    heat_flow_ability,
    material_zone_label,
    reciprocal_warming_storage,
    collector_potential_field,
    tab_indicator,
    sheet_node_link_matrix,
    solution_salt_level,
    grain_shell_level,
    solution_diffusion_matrix,
    grain_diffusion_matrix,
):
    sheets, _, span = warmth_level.shape
    shells, points, _, part = grain_shell_level.shape
    blocks = span // LANES
    nodes = points * part // LANES
    n = sheets * blocks
    edge = 2 * blocks
    size = 3 * n + edge

    def both_layers(pairs):
        return [(s * 2 + j, t * 2 + j) for s, t in pairs for j in range(2)]

    def across(where):
        return [(t * 2 + j, t * 2 + 1 - j) for t in where for j in range(2)]

    def mutual(pairs):
        return pairs + [(t, s) for s, t in pairs]

    def send(value, pairs):
        return lax.ppermute(value, ("tile", "layer"), pairs)

    cores = both_layers(mutual([(t, t + 1) for t in range(0, tiles, 2)]))
    beside = both_layers(mutual([(t, t - 1) for t in range(2, tiles, 2)]))
    beside = beside + across([0, tiles - 1])
    beyond = both_layers(mutual([(t, t - 3) for t in range(4, tiles, 2)]))
    beyond = beyond + across([0, 2, tiles - 3, tiles - 1])
    skipping = both_layers(mutual([(t, t + 3) for t in range(0, tiles - 3, 2)]))
    skipping = skipping + across([1, tiles - 2])
    layers = across(range(tiles))

    own = call(
        functools.partial(pack_kernel, blocks),
        "pack",
        shaped(3 * n + edge, LANES),
        [HBM] * 6,
        VMEM,
        1000,
        100000,
        (
            pltpu.SMEM(reciprocal_warming_storage.shape, jnp.float32),
            pltpu.VMEM((n, LANES), jnp.float32),
            pltpu.VMEM((n, LANES), jnp.int32),
            pltpu.VMEM((blocks, LANES), jnp.int32),
            pltpu.SemaphoreType.DMA((6,)),
        ),
    )(
        *in_hbm(
            reciprocal_warming_storage,
            warmth_level.reshape(n, LANES),
            heat_flow_ability.reshape(n, LANES),
            material_zone_label.reshape(n, LANES),
            collector_potential_field.reshape(n, LANES),
            tab_indicator.reshape(blocks, LANES),
        )
    )
    partner = send(own, cores)
    near = send(own, beside)
    skip = send(own, skipping)
    far = send(own[0 : 2 * n], beyond)
    held, local, factors = call(
        local_kernel,
        "columns",
        (
            shaped(shells, nodes, LANES),
            shaped(2 * nodes, LANES),
            shaped(shells, LANES),
        ),
        [HBM] * 4,
        (VMEM,) * 3,
        10**7,
        3000000,
        (
            pltpu.SMEM(grain_diffusion_matrix.shape, jnp.float32),
            pltpu.VMEM((nodes, LANES), jnp.float32),
            pltpu.VMEM(solution_diffusion_matrix.shape, jnp.float32),
            pltpu.SemaphoreType.DMA((3,)),
            pltpu.SemaphoreType.DMA((4,)),
        ),
    )(
        *in_hbm(
            grain_diffusion_matrix,
            grain_shell_level.reshape(shells, nodes, LANES),
            solution_salt_level.reshape(nodes, LANES),
            solution_diffusion_matrix,
        )
    )
    other_local = send(local, layers)
    near_in = send(near, cores)
    near, skip, far, held, local = lax.optimization_barrier((near, skip, far, held, local))
    skip_in = send(skip, cores)
    mine, masks = call(
        functools.partial(sweep_kernel, sheets, blocks, tiles),
        "sweeps",
        (shaped(2 * n + 5 * edge, LANES), shaped(5 * edge, LANES)),
        [VMEM] * 7,
        (VMEM, VMEM),
        10**6,
        500000,
    )(own, partner, near, skip, far, near_in, skip_in)
    other = send(mine, layers)
    masks, turned = lax.optimization_barrier((masks, sheet_node_link_matrix.T))
    link, turned = call(
        functools.partial(link_kernel, blocks, 2),
        "links",
        (shaped(points * blocks, 2 * n), shaped(n, points * blocks)),
        [VMEM],
        (VMEM, VMEM),
        10**6,
        100000,
    )(turned)
    held, masks, other_local = lax.optimization_barrier((held, masks, other_local))
    base = call(
        grain_kernel, "grains", shaped(shells, nodes, LANES), [VMEM] * 2, VMEM, 10**9, 3000000
    )(held, grain_diffusion_matrix)
    next_warmth, warming, flux, grain, salt = call(
        functools.partial(reaction_kernel, sheets, blocks),
        "reaction",
        (
            shaped(n, LANES),
            shaped(n, LANES),
            shaped(n, LANES),
            shaped(shells, nodes, LANES),
            shaped(nodes, LANES),
        ),
        [VMEM] * 9,
        (HBM,) * 5,
        10**7,
        3000000,
        (
            pltpu.VMEM((2 * n, 2 * LANES), jnp.float32),
            pltpu.VMEM((n, 2 * LANES), jnp.float32),
            pltpu.VMEM((shells, nodes, LANES), jnp.float32),
            pltpu.SemaphoreType.DMA((4,)),
            pltpu.SemaphoreType.DMA((4,)),
        ),
    )(factors, mine, other, local, other_local, masks, base, link, turned)
    return (
        next_warmth.reshape(warmth_level.shape),
        warming.reshape(warmth_level.shape),
        flux.reshape(warmth_level.shape),
        grain.reshape(grain_shell_level.shape),
        salt.reshape(solution_salt_level.shape),
    )


def solution(mesh):
    placed = (
        P("layer", "tile", None),
        P("layer", "tile", None),
        P("layer", "tile", None),
        P(),
        P("layer", "tile", None),
        P("tile", None),
        P(),
        P(None, "tile", "layer"),
        P(None, None, "tile", "layer"),
        P(),
        P(),
    )
    tiles, parts = mesh.shape["tile"], mesh.shape["layer"]
    plan = functools.partial(per_device, tiles) if parts == 2 else per_device_general
    return jax.shard_map(
        plan,
        mesh=mesh,
        in_specs=placed,
        out_specs=(
            P("layer", "tile", None),
            P("layer", "tile", None),
            P("layer", "tile", None),
            P(None, None, "tile", "layer"),
            P(None, "tile", "layer"),
        ),
        check_vma=False,
    )
```

```python
import functools

import jax
import jax.numpy as jnp
from jax import lax
from jax.experimental import pallas as pl
from jax.experimental.pallas import tpu as pltpu
from jax.sharding import PartitionSpec as P

SWEEPS = 3
BV_ITERS = 4


warming_advance = 0.04
damping_weight = 4.5
imposed_excitation = 0.6
shell_flux = 0.5
film_resist = 0.5

LANES = 128
ROWS = 8
LOG2 = 0.6931471805599453
HIGHEST = lax.Precision.HIGHEST


def extended(block, sides, width):
    for axis, dim in sides:
        count = lax.axis_size(axis)
        forward = [(i, i + 1) for i in range(count - 1)]
        backward = [(target, source) for source, target in forward]
        low = lax.ppermute(
            lax.slice_in_dim(block, block.shape[dim] - width, None, axis=dim), axis, forward
        )
        high = lax.ppermute(lax.slice_in_dim(block, 0, width, axis=dim), axis, backward)
        block = jnp.concatenate([low, block, high], axis=dim)
    return block


def advance_stack_vertical(
    temp_col,
    volt_col,
    sheet_node_link_matrix,
    solution_salt_level,
    grain_shell_level,
    solution_diffusion_matrix,
    grain_diffusion_matrix,
):
    highest = lax.Precision.HIGHEST
    shells = grain_diffusion_matrix.shape[0]
    node_temp = jnp.einsum("el,lxy->exy", sheet_node_link_matrix, temp_col, precision=highest)
    node_voltage = jnp.einsum("el,lxy->exy", sheet_node_link_matrix, volt_col, precision=highest)
    next_solution_level = jnp.einsum(
        "ef,fxy->exy", solution_diffusion_matrix, solution_salt_level, precision=highest
    )
    surface_base = jnp.einsum(
        "s,sexy->exy", grain_diffusion_matrix[shells - 1], grain_shell_level, precision=highest
    )
    gain = shell_flux * grain_diffusion_matrix[shells - 1, shells - 1]
    rate = 0.5 * jax.nn.sigmoid(0.3 * node_temp) * jax.nn.sigmoid(next_solution_level)
    reaction = jnp.zeros_like(node_temp)
    for iteration in range(BV_ITERS):
        surface = surface_base - gain * reaction
        overvoltage = node_voltage - jnp.tanh(surface) - film_resist * reaction
        reaction = 2.0 * rate * jnp.sinh(0.5 * overvoltage)
    surface = surface_base - gain * reaction
    source = reaction * (node_voltage - jnp.tanh(surface))
    next_grain_level = jnp.einsum(
        "st,texy->sexy", grain_diffusion_matrix, grain_shell_level, precision=highest
    )
    next_grain_level = (
        next_grain_level
        - shell_flux * grain_diffusion_matrix[:, shells - 1][:, None, None, None] * reaction[None]
    )
    reaction_warming_sheets = jnp.einsum(
        "el,exy->lxy", sheet_node_link_matrix, source, precision=highest
    )
    reaction_flux_sheets = jnp.einsum(
        "el,exy->lxy", sheet_node_link_matrix, reaction, precision=highest
    )
    return (reaction_warming_sheets, reaction_flux_sheets, next_grain_level, next_solution_level)


def four_border_faces(bordered_lattice):
    return (
        bordered_lattice[:, 2:, 1:-1]
        + bordered_lattice[:, :-2, 1:-1]
        + bordered_lattice[:, 1:-1, 2:]
        + bordered_lattice[:, 1:-1, :-2]
    )


def per_device_general(
    warmth_level,
    heat_flow_ability,
    material_zone_label,
    reciprocal_warming_storage,
    collector_potential_field,
    tab_indicator,
    sheet_node_link_matrix,
    solution_salt_level,
    grain_shell_level,
    solution_diffusion_matrix,
    grain_diffusion_matrix,
):
    stored_coulomb_limit = jnp.zeros_like(warmth_level)
    for label in range(reciprocal_warming_storage.shape[0]):
        stored_coulomb_limit = stored_coulomb_limit + jnp.where(
            material_zone_label == label, reciprocal_warming_storage[label], 0.0
        )
    bordered_lattice = extended(warmth_level, (("tile", 1), ("layer", 0)), 1)
    bordered_lattice = jnp.pad(bordered_lattice, ((0, 0), (0, 0), (1, 1)))
    neighbour_entries = bordered_lattice[2:, 1:-1, 1:-1] + bordered_lattice[:-2, 1:-1, 1:-1]
    neighbour_entries = (
        neighbour_entries + bordered_lattice[1:-1, 2:, 1:-1] + bordered_lattice[1:-1, :-2, 1:-1]
    )
    neighbour_entries = (
        neighbour_entries + bordered_lattice[1:-1, 1:-1, 2:] + bordered_lattice[1:-1, 1:-1, :-2]
    )
    next_warmth_level = (
        warmth_level
        + warming_advance
        * stored_coulomb_limit
        * heat_flow_ability
        * (neighbour_entries - 6.0 * warmth_level)
    )
    bounded_entries = (1 - tab_indicator).astype(jnp.float32)[None]
    battery_potential_drop = collector_potential_field
    for sweep in range(SWEEPS):
        enclosed_lattice = extended(battery_potential_drop, (("tile", 1),), 1)
        enclosed_lattice = jnp.pad(enclosed_lattice, ((0, 0), (0, 0), (1, 1)))
        battery_potential_drop = (
            bounded_entries
            * (four_border_faces(enclosed_lattice) + imposed_excitation * next_warmth_level)
            / damping_weight
        )
    temp_col, volt_col = (
        lax.all_to_all(next_warmth_level, "layer", split_axis=2, concat_axis=0, tiled=True),
        lax.all_to_all(battery_potential_drop, "layer", split_axis=2, concat_axis=0, tiled=True),
    )
    heat_col, current_col, next_grain_level, next_solution_level = advance_stack_vertical(
        temp_col,
        volt_col,
        sheet_node_link_matrix,
        solution_salt_level,
        grain_shell_level,
        solution_diffusion_matrix,
        grain_diffusion_matrix,
    )
    reaction_warming_sheets, reaction_flux_sheets = (
        lax.all_to_all(heat_col, "layer", split_axis=0, concat_axis=2, tiled=True),
        lax.all_to_all(current_col, "layer", split_axis=0, concat_axis=2, tiled=True),
    )
    return (
        next_warmth_level,
        reaction_warming_sheets,
        reaction_flux_sheets,
        next_grain_level,
        next_solution_level,
    )


def along_span(field, blocks):
    rows = field.shape[0]
    lane = lax.broadcasted_iota(jnp.int32, field.shape, 1)
    block = lax.rem(lax.broadcasted_iota(jnp.int32, field.shape, 0), blocks)
    low = pltpu.roll(field, 1, 1)
    low_carry = jnp.where(block == 0, 0.0, pltpu.roll(low, 1, 0))
    high = pltpu.roll(field, LANES - 1, 1)
    high_carry = jnp.where(block == blocks - 1, 0.0, pltpu.roll(high, rows - 1, 0))
    return jnp.where(lane == 0, low_carry, low) + jnp.where(lane == LANES - 1, high_carry, high)


def along_sheets(field, blocks):
    rows = field.shape[0]
    row = lax.broadcasted_iota(jnp.int32, field.shape, 0)
    low = jnp.where(row < blocks, 0.0, pltpu.roll(field, blocks, 0))
    high = jnp.where(row >= rows - blocks, 0.0, pltpu.roll(field, rows - blocks, 0))
    return low + high


def fetch(pairs, sems):
    copies = [pltpu.make_async_copy(src, dst, sems.at[i]) for i, (src, dst) in enumerate(pairs)]
    for copy in copies:
        copy.start()
    return copies


def pack_kernel(
    blocks, storage, warmth, ability, zone, potential, tab, out, regions, heat, label, tabs, sems
):
    n = warmth.shape[0]
    copies = fetch(
        (
            (storage, regions),
            (zone, label),
            (ability, heat),
            (tab, tabs),
            (warmth, out.at[0:n]),
            (potential, out.at[n : 2 * n]),
        ),
        sems,
    )
    for copy in copies[:4]:
        copy.wait()
    zones = label[...]
    capacity = jnp.full(zones.shape, regions[0])
    for region in range(1, regions.shape[0]):
        capacity = jnp.where(zones == region, regions[region], capacity)
    out[2 * n : 3 * n, :] = warming_advance * capacity * heat[...]
    free = (1 - tabs[...]).astype(jnp.float32) * (1.0 / damping_weight)
    out[3 * n : 3 * n + blocks, :] = free
    out[3 * n + blocks : 3 * n + 2 * blocks, :] = free
    for copy in copies[4:]:
        copy.wait()


def spread(count, total, per):
    row = lax.broadcasted_iota(jnp.int32, (total, count), 0)
    column = lax.broadcasted_iota(jnp.int32, (total, count), 1)
    return (row // per == column).astype(jnp.float32)


def wide(matrix, per):
    rows, columns = matrix.shape
    left = spread(rows, rows * per, per)
    right = spread(columns, columns * per, per)
    full = jnp.dot(left, matrix, precision=HIGHEST, preferred_element_type=jnp.float32)
    full = lax.dot_general(
        full, right, (((1,), (1,)), ((), ())), precision=HIGHEST, preferred_element_type=jnp.float32
    )
    row = lax.broadcasted_iota(jnp.int32, full.shape, 0)
    column = lax.broadcasted_iota(jnp.int32, full.shape, 1)
    return jnp.where(lax.rem(row, per) == lax.rem(column, per), full, 0.0)


def halves(value):
    high = value.astype(jnp.bfloat16)
    return high, (value - high.astype(jnp.float32)).astype(jnp.bfloat16)


def link_kernel(blocks, parts, turned, wide_link, wide_turned):
    sheets, points = turned.shape
    per = blocks // parts
    own = sheets // parts
    rows, columns = points * blocks, sheets * blocks
    layer = lax.axis_index("layer")
    product = functools.partial(
        lax.dot_general, precision=HIGHEST, preferred_element_type=jnp.float32
    )
    plain, across = (((1,), (0,)), ((), ())), (((1,), (1,)), ((), ()))

    def iota(shape):
        return [lax.broadcasted_iota(jnp.int32, shape, axis) for axis in range(2)]

    def fits(r, c):
        part = lax.rem(r // (points * per) + layer, parts)
        return lax.rem(c, blocks) == part * per + lax.rem(r, per)

    r, c = iota((rows, points))
    pick = (lax.rem(r, points * per) // per == c).astype(jnp.float32)
    r, c = iota((sheets, columns))
    split = (c // blocks == r).astype(jnp.float32)
    full = product(product(pick, turned[...], across), split, plain)
    r, c = iota((rows, columns))
    wide_link[...] = jnp.where(fits(r, c), full, 0.0)
    r, c = iota((own * blocks, sheets))
    split = (r // blocks + own * layer == c).astype(jnp.float32)
    full = product(product(split, turned[...], plain), pick, across)
    r, c = iota((own * blocks, rows))
    wide_turned[...] = jnp.where(fits(c, r), full, 0.0)


def local_kernel(
    diffusion,
    grain,
    salt,
    salt_matrix,
    held,
    local,
    factors,
    weights,
    level,
    matrix,
    sems,
    grain_sems,
):
    shells, nodes, _ = grain.shape
    part = shells // grain_sems.shape[0]
    small = fetch(((salt, level), (salt_matrix, matrix), (diffusion, weights)), sems)
    copies = fetch(
        [(grain.at[s : s + part], held.at[s : s + part]) for s in range(0, shells, part)],
        grain_sems,
    )
    for copy in small:
        copy.wait()
    points = matrix.shape[0]
    per = nodes // points
    spans = [level[pl.ds(i, points, stride=per), :] for i in range(per)]
    spans = jnp.dot(
        matrix[...],
        jnp.concatenate(spans, axis=1),
        precision=HIGHEST,
        preferred_element_type=jnp.float32,
    )
    for i in range(per):
        local[pl.ds(nodes + i, points, stride=per), :] = spans[:, i * LANES : (i + 1) * LANES]
    for shell in range(shells):
        factors[shell : shell + 1, :] = jnp.full(
            (1, LANES), shell_flux * weights[shell, shells - 1]
        )
    surface = jnp.zeros((nodes, LANES), jnp.float32)
    for i, copy in enumerate(copies):
        copy.wait()
        for shell in range(i * part, (i + 1) * part):
            surface = surface + weights[shells - 1, shell] * held[shell]
    local[0:nodes, :] = surface


def grain_kernel(grain, weights, base):
    shells, count, _ = grain.shape
    matrix_high, matrix_low = halves(wide(weights[...], ROWS))
    for start in range(0, count, 2 * ROWS):
        pair = [
            grain[:, start + k * ROWS : start + (k + 1) * ROWS, :].reshape(shells * ROWS, LANES)
            for k in range(2)
        ]
        high, low = halves(jnp.concatenate(pair, axis=1))
        dot = functools.partial(jnp.dot, preferred_element_type=jnp.float32)
        result = dot(matrix_high, high) + (dot(matrix_high, low) + dot(matrix_low, high))
        for k in range(2):
            part = result[:, k * LANES : (k + 1) * LANES].reshape(shells, ROWS, LANES)
            base[:, start + k * ROWS : start + (k + 1) * ROWS, :] = part


def sweep_kernel(
    sheets, blocks, tiles, own, partner, near, skip, far, near_in, skip_in, out, masks
):
    n = sheets * blocks
    tile = lax.axis_index("tile")
    block = lax.axis_index("layer")
    first = jnp.logical_or(tile == 0, tile == tiles - 1)
    second = jnp.logical_or(tile == 2, tile == tiles - 3)
    beside = jnp.logical_or(tile == 1, tile == tiles - 2)
    keep_outer = jnp.where(first, 0.0, 1.0)
    keep_far = jnp.where(jnp.logical_or(first, second), 0.0, 1.0)
    keep_inner = jnp.where(beside, 0.0, 1.0)

    def load(ref, start, rows, keep=None):
        value = ref[start : start + rows, :]
        return value if keep is None else keep * value

    def window(start, rows):
        return [
            load(skip_in, start, rows, keep_outer),
            load(near, start, rows, keep_outer),
            load(own, start, rows),
            load(partner, start, rows),
            load(near_in, start, rows, keep_inner),
        ]

    warmth = [load(far, 0, n, keep_far)] + window(0, n) + [load(skip, 0, n, keep_inner)]
    volt = [load(far, n, n, keep_far)] + window(n, n) + [load(skip, n, n, keep_inner)]
    slope = window(2 * n, n)
    free = window(3 * n, 2 * blocks)
    for i in range(5):
        masks[2 * i * blocks : 2 * (i + 1) * blocks, :] = free[i]
    free = [jnp.concatenate([m] * (n // m.shape[0]), axis=0) for m in free]
    temp = []
    for i in range(5):
        w = warmth[i + 1]
        around = warmth[i] + warmth[i + 2] + along_sheets(w, blocks) + along_span(w, blocks)
        temp.append(w + slope[i] * (around - 6.0 * w))
    for sweep in range(SWEEPS):
        volt = [
            free[i + sweep]
            * (
                volt[i]
                + volt[i + 2]
                + along_span(volt[i + 1], blocks)
                + imposed_excitation * temp[i + sweep]
            )
            for i in range(len(volt) - 2)
        ]
    out[0:n, :] = temp[2]
    out[n : 2 * n, :] = volt[0]
    for i in range(5):
        for k, value in enumerate((warmth[i + 1], slope[i])):
            edge = jnp.where(block == 0, value[n - blocks :, :], value[0:blocks, :])
            start = 2 * n + (2 * i + k) * blocks
            out[start : start + blocks, :] = edge


def react(surface_base, gain, rate, node_voltage):
    reaction = jnp.zeros_like(node_voltage)
    for iteration in range(BV_ITERS):
        surface = surface_base - gain * reaction
        half = 0.5 * (node_voltage - jnp.tanh(surface) - film_resist * reaction)
        reaction = rate * (jnp.exp(half - LOG2) - jnp.exp(-half - LOG2))
    surface = surface_base - gain * reaction
    return reaction, reaction * (node_voltage - jnp.tanh(surface))


def reaction_kernel(
    sheets,
    blocks,
    factors,
    mine,
    other,
    local,
    other_local,
    masks,
    base,
    link,
    turned,
    next_warmth,
    warming,
    flux,
    grain_out,
    salt_out,
    both,
    sheets_now,
    copy_out,
    sems,
    grain_sems,
):
    n = sheets * blocks
    shells, nodes, _ = base.shape
    block = lax.axis_index("layer")
    edge = 2 * blocks
    early = fetch(((local.at[nodes : 2 * nodes], salt_out),), sems)

    free = [masks[i * edge : (i + 1) * edge, :] for i in range(5)]
    added = []
    for i in range(5):
        at = 2 * n + i * edge
        added.append(pltpu.roll(mine[at : at + edge, :], blocks, 0) * other[at : at + edge, :])
    volt = [free[i] * (imposed_excitation * added[i]) for i in range(5)]
    for sweep in range(1, SWEEPS):
        volt = [
            free[i + sweep]
            * (
                volt[i]
                + volt[i + 2]
                + along_span(volt[i + 1], blocks)
                + imposed_excitation * added[i + sweep]
            )
            for i in range(len(volt) - 2)
        ]
    here = pl.ds(pl.multiple_of(block * n, ROWS), n)
    there = pl.ds(pl.multiple_of((1 - block) * n, ROWS), n)
    both[here, 0:LANES] = mine[0:n, :]
    both[there, 0:LANES] = other[0:n, :]
    both[here, LANES:] = mine[n : 2 * n, :]
    both[there, LANES:] = other[n : 2 * n, :]
    extra = jnp.concatenate([added[2], volt[0]], axis=1)
    extra = jnp.where(block == 0, extra, pltpu.roll(extra, blocks, 0))
    both[n - blocks : n + blocks, :] += extra
    warmth_copy = pltpu.make_async_copy(both.at[here, 0:LANES], next_warmth, sems.at[1])
    warmth_copy.start()

    dot = functools.partial(jnp.dot, precision=HIGHEST, preferred_element_type=jnp.float32)
    node = dot(link[...], both[...])
    gain = factors[shells - 1 :, :]
    surface_base = jnp.concatenate([local[0:nodes, :], other_local[0:nodes, :]], axis=0)
    salt = jnp.concatenate(
        [local[nodes : 2 * nodes, :], other_local[nodes : 2 * nodes, :]], axis=0
    )
    rate = (1.0 / (1.0 + jnp.exp(-0.3 * node[:, 0:LANES]))) * (1.0 / (1.0 + jnp.exp(-salt)))
    reaction, source = react(surface_base, gain, rate, node[:, LANES:])
    link_high, link_low = halves(turned[...])
    high, low = halves(jnp.concatenate([source, reaction], axis=1))
    short = functools.partial(jnp.dot, preferred_element_type=jnp.float32)
    sheets_now[...] = short(link_high, high) + (short(link_high, low) + short(link_low, high))
    late = [
        pltpu.make_async_copy(sheets_now.at[:, 0:LANES], warming, sems.at[2]),
        pltpu.make_async_copy(sheets_now.at[:, LANES:], flux, sems.at[3]),
    ]
    for copy in late:
        copy.start()
    copies = []
    step = shells // grain_sems.shape[0]
    for first in range(0, shells, step):
        for shell in range(first, first + step):
            factor = factors[shell : shell + 1, :]
            copy_out[shell] = base[shell] - factor * reaction[0:nodes, :]
        copies.append(
            pltpu.make_async_copy(
                copy_out.at[first : first + step],
                grain_out.at[first : first + step],
                grain_sems.at[first // step],
            )
        )
        copies[-1].start()
    for copy in early + [warmth_copy] + copies + late:
        copy.wait()


VMEM = pl.BlockSpec(memory_space=pltpu.VMEM)
SMEM = pl.BlockSpec(memory_space=pltpu.SMEM)
HBM = pl.BlockSpec(memory_space=pltpu.HBM)


def in_hbm(*values):
    return [pltpu.with_memory_space_constraint(value, pltpu.HBM) for value in values]


def shaped(*shape):
    return jax.ShapeDtypeStruct(shape, jnp.float32)


def call(kernel, name, out, ins, outs, flops, nbytes, scratch=()):
    return pl.pallas_call(
        kernel,
        out_shape=out,
        in_specs=ins,
        out_specs=outs,
        scratch_shapes=scratch,
        compiler_params=pltpu.CompilerParams(vmem_limit_bytes=32 * 1024 * 1024),
        cost_estimate=pl.CostEstimate(flops=flops, bytes_accessed=nbytes, transcendentals=0),
        name=name,
    )


def per_device(
    tiles,
    warmth_level,
    heat_flow_ability,
    material_zone_label,
    reciprocal_warming_storage,
    collector_potential_field,
    tab_indicator,
    sheet_node_link_matrix,
    solution_salt_level,
    grain_shell_level,
    solution_diffusion_matrix,
    grain_diffusion_matrix,
):
    sheets, _, span = warmth_level.shape
    shells, points, _, part = grain_shell_level.shape
    blocks = span // LANES
    nodes = points * part // LANES
    n = sheets * blocks
    edge = 2 * blocks
    size = 3 * n + edge

    def both_layers(pairs):
        return [(s * 2 + j, t * 2 + j) for s, t in pairs for j in range(2)]

    def across(where):
        return [(t * 2 + j, t * 2 + 1 - j) for t in where for j in range(2)]

    def mutual(pairs):
        return pairs + [(t, s) for s, t in pairs]

    def send(value, pairs):
        return lax.ppermute(value, ("tile", "layer"), pairs)

    cores = both_layers(mutual([(t, t + 1) for t in range(0, tiles, 2)]))
    beside = both_layers(mutual([(t, t - 1) for t in range(2, tiles, 2)]))
    beside = beside + across([0, tiles - 1])
    beyond = both_layers(mutual([(t, t - 3) for t in range(4, tiles, 2)]))
    beyond = beyond + across([0, 2, tiles - 3, tiles - 1])
    skipping = both_layers(mutual([(t, t + 3) for t in range(0, tiles - 3, 2)]))
    skipping = skipping + across([1, tiles - 2])
    layers = across(range(tiles))

    own = call(
        functools.partial(pack_kernel, blocks),
        "pack",
        shaped(3 * n + edge, LANES),
        [HBM] * 6,
        VMEM,
        1000,
        100000,
        (
            pltpu.SMEM(reciprocal_warming_storage.shape, jnp.float32),
            pltpu.VMEM((n, LANES), jnp.float32),
            pltpu.VMEM((n, LANES), jnp.int32),
            pltpu.VMEM((blocks, LANES), jnp.int32),
            pltpu.SemaphoreType.DMA((6,)),
        ),
    )(
        *in_hbm(
            reciprocal_warming_storage,
            warmth_level.reshape(n, LANES),
            heat_flow_ability.reshape(n, LANES),
            material_zone_label.reshape(n, LANES),
            collector_potential_field.reshape(n, LANES),
            tab_indicator.reshape(blocks, LANES),
        )
    )
    partner = send(own, cores)
    near = send(own, beside)
    skip = send(own, skipping)
    far = send(own[0 : 2 * n], beyond)
    held, local, factors = call(
        local_kernel,
        "columns",
        (
            shaped(shells, nodes, LANES),
            shaped(2 * nodes, LANES),
            shaped(shells, LANES),
        ),
        [HBM] * 4,
        (VMEM,) * 3,
        10**7,
        3000000,
        (
            pltpu.SMEM(grain_diffusion_matrix.shape, jnp.float32),
            pltpu.VMEM((nodes, LANES), jnp.float32),
            pltpu.VMEM(solution_diffusion_matrix.shape, jnp.float32),
            pltpu.SemaphoreType.DMA((3,)),
            pltpu.SemaphoreType.DMA((4,)),
        ),
    )(
        *in_hbm(
            grain_diffusion_matrix,
            grain_shell_level.reshape(shells, nodes, LANES),
            solution_salt_level.reshape(nodes, LANES),
            solution_diffusion_matrix,
        )
    )
    other_local = send(local, layers)
    near_in = send(near, cores)
    near, skip, far, held, local = lax.optimization_barrier((near, skip, far, held, local))
    skip_in = send(skip, cores)
    mine, masks = call(
        functools.partial(sweep_kernel, sheets, blocks, tiles),
        "sweeps",
        (shaped(2 * n + 5 * edge, LANES), shaped(5 * edge, LANES)),
        [VMEM] * 7,
        (VMEM, VMEM),
        10**6,
        500000,
    )(own, partner, near, skip, far, near_in, skip_in)
    other = send(mine, layers)
    masks, turned = lax.optimization_barrier((masks, sheet_node_link_matrix.T))
    link, turned = call(
        functools.partial(link_kernel, blocks, 2),
        "links",
        (shaped(points * blocks, 2 * n), shaped(n, points * blocks)),
        [VMEM],
        (VMEM, VMEM),
        10**6,
        100000,
    )(turned)
    held, masks, other_local = lax.optimization_barrier((held, masks, other_local))
    base = call(
        grain_kernel, "grains", shaped(shells, nodes, LANES), [VMEM] * 2, VMEM, 10**9, 3000000
    )(held, grain_diffusion_matrix)
    next_warmth, warming, flux, grain, salt = call(
        functools.partial(reaction_kernel, sheets, blocks),
        "reaction",
        (
            shaped(n, LANES),
            shaped(n, LANES),
            shaped(n, LANES),
            shaped(shells, nodes, LANES),
            shaped(nodes, LANES),
        ),
        [VMEM] * 9,
        (HBM,) * 5,
        10**7,
        3000000,
        (
            pltpu.VMEM((2 * n, 2 * LANES), jnp.float32),
            pltpu.VMEM((n, 2 * LANES), jnp.float32),
            pltpu.VMEM((shells, nodes, LANES), jnp.float32),
            pltpu.SemaphoreType.DMA((4,)),
            pltpu.SemaphoreType.DMA((4,)),
        ),
    )(factors, mine, other, local, other_local, masks, base, link, turned)
    return (
        next_warmth.reshape(warmth_level.shape),
        warming.reshape(warmth_level.shape),
        flux.reshape(warmth_level.shape),
        grain.reshape(grain_shell_level.shape),
        salt.reshape(solution_salt_level.shape),
    )


def solution(mesh):
    placed = (
        P("layer", "tile", None),
        P("layer", "tile", None),
        P("layer", "tile", None),
        P(),
        P("layer", "tile", None),
        P("tile", None),
        P(),
        P(None, "tile", "layer"),
        P(None, None, "tile", "layer"),
        P(),
        P(),
    )
    tiles, parts = mesh.shape["tile"], mesh.shape["layer"]
    plan = functools.partial(per_device, tiles) if parts == 2 else per_device_general
    return jax.shard_map(
        plan,
        mesh=mesh,
        in_specs=placed,
        out_specs=(
            P("layer", "tile", None),
            P("layer", "tile", None),
            P("layer", "tile", None),
            P(None, None, "tile", "layer"),
            P(None, "tile", "layer"),
        ),
        check_vma=False,
    )
```

```python
import functools

import jax
import jax.numpy as jnp
from jax import lax
from jax.experimental import pallas as pl
from jax.experimental.pallas import tpu as pltpu
from jax.sharding import PartitionSpec as P

SWEEPS = 3
BV_ITERS = 4


warming_advance = 0.04
damping_weight = 4.5
imposed_excitation = 0.6
shell_flux = 0.5
film_resist = 0.5

LANES = 128
ROWS = 8
LOG2 = 0.6931471805599453
HIGHEST = lax.Precision.HIGHEST


def extended(block, sides, width):
    for axis, dim in sides:
        count = lax.axis_size(axis)
        forward = [(i, i + 1) for i in range(count - 1)]
        backward = [(target, source) for source, target in forward]
        low = lax.ppermute(
            lax.slice_in_dim(block, block.shape[dim] - width, None, axis=dim), axis, forward
        )
        high = lax.ppermute(lax.slice_in_dim(block, 0, width, axis=dim), axis, backward)
        block = jnp.concatenate([low, block, high], axis=dim)
    return block


def advance_stack_vertical(
    temp_col,
    volt_col,
    sheet_node_link_matrix,
    solution_salt_level,
    grain_shell_level,
    solution_diffusion_matrix,
    grain_diffusion_matrix,
):
    highest = lax.Precision.HIGHEST
    shells = grain_diffusion_matrix.shape[0]
    node_temp = jnp.einsum("el,lxy->exy", sheet_node_link_matrix, temp_col, precision=highest)
    node_voltage = jnp.einsum("el,lxy->exy", sheet_node_link_matrix, volt_col, precision=highest)
    next_solution_level = jnp.einsum(
        "ef,fxy->exy", solution_diffusion_matrix, solution_salt_level, precision=highest
    )
    surface_base = jnp.einsum(
        "s,sexy->exy", grain_diffusion_matrix[shells - 1], grain_shell_level, precision=highest
    )
    gain = shell_flux * grain_diffusion_matrix[shells - 1, shells - 1]
    rate = 0.5 * jax.nn.sigmoid(0.3 * node_temp) * jax.nn.sigmoid(next_solution_level)
    reaction = jnp.zeros_like(node_temp)
    for iteration in range(BV_ITERS):
        surface = surface_base - gain * reaction
        overvoltage = node_voltage - jnp.tanh(surface) - film_resist * reaction
        reaction = 2.0 * rate * jnp.sinh(0.5 * overvoltage)
    surface = surface_base - gain * reaction
    source = reaction * (node_voltage - jnp.tanh(surface))
    next_grain_level = jnp.einsum(
        "st,texy->sexy", grain_diffusion_matrix, grain_shell_level, precision=highest
    )
    next_grain_level = (
        next_grain_level
        - shell_flux * grain_diffusion_matrix[:, shells - 1][:, None, None, None] * reaction[None]
    )
    reaction_warming_sheets = jnp.einsum(
        "el,exy->lxy", sheet_node_link_matrix, source, precision=highest
    )
    reaction_flux_sheets = jnp.einsum(
        "el,exy->lxy", sheet_node_link_matrix, reaction, precision=highest
    )
    return (reaction_warming_sheets, reaction_flux_sheets, next_grain_level, next_solution_level)


def four_border_faces(bordered_lattice):
    return (
        bordered_lattice[:, 2:, 1:-1]
        + bordered_lattice[:, :-2, 1:-1]
        + bordered_lattice[:, 1:-1, 2:]
        + bordered_lattice[:, 1:-1, :-2]
    )


def per_device_general(
    warmth_level,
    heat_flow_ability,
    material_zone_label,
    reciprocal_warming_storage,
    collector_potential_field,
    tab_indicator,
    sheet_node_link_matrix,
    solution_salt_level,
    grain_shell_level,
    solution_diffusion_matrix,
    grain_diffusion_matrix,
):
    stored_coulomb_limit = jnp.zeros_like(warmth_level)
    for label in range(reciprocal_warming_storage.shape[0]):
        stored_coulomb_limit = stored_coulomb_limit + jnp.where(
            material_zone_label == label, reciprocal_warming_storage[label], 0.0
        )
    bordered_lattice = extended(warmth_level, (("tile", 1), ("layer", 0)), 1)
    bordered_lattice = jnp.pad(bordered_lattice, ((0, 0), (0, 0), (1, 1)))
    neighbour_entries = bordered_lattice[2:, 1:-1, 1:-1] + bordered_lattice[:-2, 1:-1, 1:-1]
    neighbour_entries = (
        neighbour_entries + bordered_lattice[1:-1, 2:, 1:-1] + bordered_lattice[1:-1, :-2, 1:-1]
    )
    neighbour_entries = (
        neighbour_entries + bordered_lattice[1:-1, 1:-1, 2:] + bordered_lattice[1:-1, 1:-1, :-2]
    )
    next_warmth_level = (
        warmth_level
        + warming_advance
        * stored_coulomb_limit
        * heat_flow_ability
        * (neighbour_entries - 6.0 * warmth_level)
    )
    bounded_entries = (1 - tab_indicator).astype(jnp.float32)[None]
    battery_potential_drop = collector_potential_field
    for sweep in range(SWEEPS):
        enclosed_lattice = extended(battery_potential_drop, (("tile", 1),), 1)
        enclosed_lattice = jnp.pad(enclosed_lattice, ((0, 0), (0, 0), (1, 1)))
        battery_potential_drop = (
            bounded_entries
            * (four_border_faces(enclosed_lattice) + imposed_excitation * next_warmth_level)
            / damping_weight
        )
    temp_col, volt_col = (
        lax.all_to_all(next_warmth_level, "layer", split_axis=2, concat_axis=0, tiled=True),
        lax.all_to_all(battery_potential_drop, "layer", split_axis=2, concat_axis=0, tiled=True),
    )
    heat_col, current_col, next_grain_level, next_solution_level = advance_stack_vertical(
        temp_col,
        volt_col,
        sheet_node_link_matrix,
        solution_salt_level,
        grain_shell_level,
        solution_diffusion_matrix,
        grain_diffusion_matrix,
    )
    reaction_warming_sheets, reaction_flux_sheets = (
        lax.all_to_all(heat_col, "layer", split_axis=0, concat_axis=2, tiled=True),
        lax.all_to_all(current_col, "layer", split_axis=0, concat_axis=2, tiled=True),
    )
    return (
        next_warmth_level,
        reaction_warming_sheets,
        reaction_flux_sheets,
        next_grain_level,
        next_solution_level,
    )


def along_span(field, blocks):
    rows = field.shape[0]
    lane = lax.broadcasted_iota(jnp.int32, field.shape, 1)
    block = lax.rem(lax.broadcasted_iota(jnp.int32, field.shape, 0), blocks)
    low = pltpu.roll(field, 1, 1)
    low_carry = jnp.where(block == 0, 0.0, pltpu.roll(low, 1, 0))
    high = pltpu.roll(field, LANES - 1, 1)
    high_carry = jnp.where(block == blocks - 1, 0.0, pltpu.roll(high, rows - 1, 0))
    return jnp.where(lane == 0, low_carry, low) + jnp.where(lane == LANES - 1, high_carry, high)


def along_sheets(field, blocks):
    rows = field.shape[0]
    row = lax.broadcasted_iota(jnp.int32, field.shape, 0)
    low = jnp.where(row < blocks, 0.0, pltpu.roll(field, blocks, 0))
    high = jnp.where(row >= rows - blocks, 0.0, pltpu.roll(field, rows - blocks, 0))
    return low + high


def fetch(pairs, sems):
    copies = [pltpu.make_async_copy(src, dst, sems.at[i]) for i, (src, dst) in enumerate(pairs)]
    for copy in copies:
        copy.start()
    return copies


def pack_kernel(
    blocks, storage, warmth, ability, zone, potential, tab, out, regions, heat, label, tabs, sems
):
    n = warmth.shape[0]
    copies = fetch(
        (
            (storage, regions),
            (zone, label),
            (ability, heat),
            (tab, tabs),
            (warmth, out.at[0:n]),
            (potential, out.at[n : 2 * n]),
        ),
        sems,
    )
    for copy in copies[:4]:
        copy.wait()
    zones = label[...]
    capacity = jnp.full(zones.shape, regions[0])
    for region in range(1, regions.shape[0]):
        capacity = jnp.where(zones == region, regions[region], capacity)
    out[2 * n : 3 * n, :] = warming_advance * capacity * heat[...]
    free = (1 - tabs[...]).astype(jnp.float32) * (1.0 / damping_weight)
    out[3 * n : 3 * n + blocks, :] = free
    out[3 * n + blocks : 3 * n + 2 * blocks, :] = free
    for copy in copies[4:]:
        copy.wait()


def spread(count, total, per):
    row = lax.broadcasted_iota(jnp.int32, (total, count), 0)
    column = lax.broadcasted_iota(jnp.int32, (total, count), 1)
    return (row // per == column).astype(jnp.float32)


def wide(matrix, per):
    rows, columns = matrix.shape
    left = spread(rows, rows * per, per)
    right = spread(columns, columns * per, per)
    full = jnp.dot(left, matrix, precision=HIGHEST, preferred_element_type=jnp.float32)
    full = lax.dot_general(
        full, right, (((1,), (1,)), ((), ())), precision=HIGHEST, preferred_element_type=jnp.float32
    )
    row = lax.broadcasted_iota(jnp.int32, full.shape, 0)
    column = lax.broadcasted_iota(jnp.int32, full.shape, 1)
    return jnp.where(lax.rem(row, per) == lax.rem(column, per), full, 0.0)


def halves(value):
    high = value.astype(jnp.bfloat16)
    return high, (value - high.astype(jnp.float32)).astype(jnp.bfloat16)


def link_kernel(blocks, parts, turned, wide_link, wide_turned):
    sheets, points = turned.shape
    per = blocks // parts
    own = sheets // parts
    rows, columns = points * blocks, sheets * blocks
    layer = lax.axis_index("layer")
    product = functools.partial(
        lax.dot_general, precision=HIGHEST, preferred_element_type=jnp.float32
    )
    plain, across = (((1,), (0,)), ((), ())), (((1,), (1,)), ((), ()))

    def iota(shape):
        return [lax.broadcasted_iota(jnp.int32, shape, axis) for axis in range(2)]

    def fits(r, c):
        part = lax.rem(r // (points * per) + layer, parts)
        return lax.rem(c, blocks) == part * per + lax.rem(r, per)

    r, c = iota((rows, points))
    pick = (lax.rem(r, points * per) // per == c).astype(jnp.float32)
    r, c = iota((sheets, columns))
    split = (c // blocks == r).astype(jnp.float32)
    full = product(product(pick, turned[...], across), split, plain)
    r, c = iota((rows, columns))
    wide_link[...] = jnp.where(fits(r, c), full, 0.0)
    r, c = iota((own * blocks, sheets))
    split = (r // blocks + own * layer == c).astype(jnp.float32)
    full = product(product(split, turned[...], plain), pick, across)
    r, c = iota((own * blocks, rows))
    wide_turned[...] = jnp.where(fits(c, r), full, 0.0)


def local_kernel(
    diffusion,
    grain,
    salt,
    salt_matrix,
    held,
    local,
    factors,
    weights,
    level,
    matrix,
    sems,
    grain_sems,
):
    shells, nodes, _ = grain.shape
    part = shells // grain_sems.shape[0]
    small = fetch(((salt, level), (salt_matrix, matrix), (diffusion, weights)), sems)
    copies = fetch(
        [(grain.at[s : s + part], held.at[s : s + part]) for s in range(0, shells, part)],
        grain_sems,
    )
    for copy in small:
        copy.wait()
    points = matrix.shape[0]
    per = nodes // points
    spans = [level[pl.ds(i, points, stride=per), :] for i in range(per)]
    spans = jnp.dot(
        matrix[...],
        jnp.concatenate(spans, axis=1),
        precision=HIGHEST,
        preferred_element_type=jnp.float32,
    )
    for i in range(per):
        local[pl.ds(nodes + i, points, stride=per), :] = spans[:, i * LANES : (i + 1) * LANES]
    for shell in range(shells):
        factors[shell : shell + 1, :] = jnp.full(
            (1, LANES), shell_flux * weights[shell, shells - 1]
        )
    surface = jnp.zeros((nodes, LANES), jnp.float32)
    for i, copy in enumerate(copies):
        copy.wait()
        for shell in range(i * part, (i + 1) * part):
            surface = surface + weights[shells - 1, shell] * held[shell]
    local[0:nodes, :] = surface


def grain_kernel(grain, weights, base):
    shells, count, _ = grain.shape
    matrix_high, matrix_low = halves(wide(weights[...], ROWS))
    for start in range(0, count, 2 * ROWS):
        pair = [
            grain[:, start + k * ROWS : start + (k + 1) * ROWS, :].reshape(shells * ROWS, LANES)
            for k in range(2)
        ]
        high, low = halves(jnp.concatenate(pair, axis=1))
        dot = functools.partial(jnp.dot, preferred_element_type=jnp.float32)
        result = dot(matrix_high, high) + (dot(matrix_high, low) + dot(matrix_low, high))
        for k in range(2):
            part = result[:, k * LANES : (k + 1) * LANES].reshape(shells, ROWS, LANES)
            base[:, start + k * ROWS : start + (k + 1) * ROWS, :] = part


def sweep_kernel(
    sheets,
    blocks,
    tiles,
    own,
    partner,
    near,
    skip,
    far,
    near_in,
    skip_in,
    far_in,
    mine,
    theirs,
    masks,
):
    n = sheets * blocks
    edge = 2 * blocks
    tile = lax.axis_index("tile")
    block = lax.axis_index("layer")
    other = tile + 1 - 2 * lax.rem(tile, 2)

    def ends(t):
        return jnp.logical_or(t == 0, t == tiles - 1)

    def near_ends(t):
        return jnp.logical_or(ends(t), jnp.logical_or(t == 2, t == tiles - 3))

    keep = [jnp.where(test(t), 0.0, 1.0) for t in (tile, other) for test in (ends, near_ends)]

    def window(start, rows, width):
        rows = slice(start, start + rows)
        values = [
            keep[1] * far[rows, :] if width == 8 else None,
            keep[0] * skip_in[rows, :],
            keep[0] * near[rows, :],
            own[rows, :],
            partner[rows, :],
            keep[2] * near_in[rows, :],
            keep[2] * skip[rows, :],
            keep[3] * far_in[rows, :] if width == 8 else None,
        ]
        return [value for value in values if value is not None]

    warmth = window(0, n, 8)
    volt = window(n, n, 8)
    slope = window(2 * n, n, 6)
    free = window(3 * n, edge, 6)
    for i in range(5):
        masks[i * edge : (i + 1) * edge, :] = free[i]
    free = [jnp.concatenate([m] * (n // edge), axis=0) for m in free]
    temp = []
    for i in range(6):
        w = warmth[i + 1]
        around = warmth[i] + warmth[i + 2] + along_sheets(w, blocks) + along_span(w, blocks)
        temp.append(w + slope[i] * (around - 6.0 * w))
    for sweep in range(SWEEPS):
        volt = [
            free[i + sweep]
            * (
                volt[i]
                + volt[i + 2]
                + along_span(volt[i + 1], blocks)
                + imposed_excitation * temp[i + sweep]
            )
            for i in range(len(volt) - 2)
        ]
    edges = [
        jnp.concatenate(
            [
                jnp.where(block == 0, value[n - blocks :, :], value[0:blocks, :])
                for value in (warmth[i + 1], slope[i])
            ],
            axis=0,
        )
        for i in range(6)
    ]
    for out, order in ((mine, range(5)), (theirs, range(5, 0, -1))):
        side = 0 if out is mine else 1
        out[0:n, :] = temp[2 + side]
        out[n : 2 * n, :] = volt[side]
        for i, at in enumerate(order):
            out[2 * n + i * edge : 2 * n + (i + 1) * edge, :] = edges[at]


def react(surface_base, gain, rate, node_voltage):
    reaction = jnp.zeros_like(node_voltage)
    for iteration in range(BV_ITERS):
        surface = surface_base - gain * reaction
        half = 0.5 * (node_voltage - jnp.tanh(surface) - film_resist * reaction)
        reaction = rate * (jnp.exp(half - LOG2) - jnp.exp(-half - LOG2))
    surface = surface_base - gain * reaction
    return reaction, reaction * (node_voltage - jnp.tanh(surface))


def reaction_kernel(
    sheets,
    blocks,
    factors,
    mine,
    other,
    local,
    other_local,
    masks,
    base,
    link,
    turned,
    next_warmth,
    warming,
    flux,
    grain_out,
    salt_out,
    both,
    sheets_now,
    copy_out,
    sems,
    grain_sems,
):
    n = sheets * blocks
    shells, nodes, _ = base.shape
    block = lax.axis_index("layer")
    edge = 2 * blocks
    early = fetch(((local.at[nodes : 2 * nodes], salt_out),), sems)

    free = [masks[i * edge : (i + 1) * edge, :] for i in range(5)]
    added = []
    for i in range(5):
        at = 2 * n + i * edge
        added.append(pltpu.roll(mine[at : at + edge, :], blocks, 0) * other[at : at + edge, :])
    volt = [free[i] * (imposed_excitation * added[i]) for i in range(5)]
    for sweep in range(1, SWEEPS):
        volt = [
            free[i + sweep]
            * (
                volt[i]
                + volt[i + 2]
                + along_span(volt[i + 1], blocks)
                + imposed_excitation * added[i + sweep]
            )
            for i in range(len(volt) - 2)
        ]
    here = pl.ds(pl.multiple_of(block * n, ROWS), n)
    there = pl.ds(pl.multiple_of((1 - block) * n, ROWS), n)
    both[here, 0:LANES] = mine[0:n, :]
    both[there, 0:LANES] = other[0:n, :]
    both[here, LANES:] = mine[n : 2 * n, :]
    both[there, LANES:] = other[n : 2 * n, :]
    extra = jnp.concatenate([added[2], volt[0]], axis=1)
    extra = jnp.where(block == 0, extra, pltpu.roll(extra, blocks, 0))
    both[n - blocks : n + blocks, :] += extra
    warmth_copy = pltpu.make_async_copy(both.at[here, 0:LANES], next_warmth, sems.at[1])
    warmth_copy.start()

    dot = functools.partial(jnp.dot, precision=HIGHEST, preferred_element_type=jnp.float32)
    node = dot(link[...], both[...])
    gain = factors[shells - 1 :, :]
    surface_base = jnp.concatenate([local[0:nodes, :], other_local[0:nodes, :]], axis=0)
    salt = jnp.concatenate(
        [local[nodes : 2 * nodes, :], other_local[nodes : 2 * nodes, :]], axis=0
    )
    rate = (1.0 / (1.0 + jnp.exp(-0.3 * node[:, 0:LANES]))) * (1.0 / (1.0 + jnp.exp(-salt)))
    reaction, source = react(surface_base, gain, rate, node[:, LANES:])
    link_high, link_low = halves(turned[...])
    high, low = halves(jnp.concatenate([source, reaction], axis=1))
    short = functools.partial(jnp.dot, preferred_element_type=jnp.float32)
    sheets_now[...] = short(link_high, high) + (short(link_high, low) + short(link_low, high))
    late = [
        pltpu.make_async_copy(sheets_now.at[:, 0:LANES], warming, sems.at[2]),
        pltpu.make_async_copy(sheets_now.at[:, LANES:], flux, sems.at[3]),
    ]
    for copy in late:
        copy.start()
    copies = []
    step = shells // grain_sems.shape[0]
    for first in range(0, shells, step):
        for shell in range(first, first + step):
            factor = factors[shell : shell + 1, :]
            copy_out[shell] = base[shell] - factor * reaction[0:nodes, :]
        copies.append(
            pltpu.make_async_copy(
                copy_out.at[first : first + step],
                grain_out.at[first : first + step],
                grain_sems.at[first // step],
            )
        )
        copies[-1].start()
    for copy in early + [warmth_copy] + copies + late:
        copy.wait()


VMEM = pl.BlockSpec(memory_space=pltpu.VMEM)
SMEM = pl.BlockSpec(memory_space=pltpu.SMEM)
HBM = pl.BlockSpec(memory_space=pltpu.HBM)


def in_hbm(*values):
    return [pltpu.with_memory_space_constraint(value, pltpu.HBM) for value in values]


def shaped(*shape):
    return jax.ShapeDtypeStruct(shape, jnp.float32)


def call(kernel, name, out, ins, outs, flops, nbytes, scratch=()):
    return pl.pallas_call(
        kernel,
        out_shape=out,
        in_specs=ins,
        out_specs=outs,
        scratch_shapes=scratch,
        compiler_params=pltpu.CompilerParams(vmem_limit_bytes=32 * 1024 * 1024),
        cost_estimate=pl.CostEstimate(flops=flops, bytes_accessed=nbytes, transcendentals=0),
        name=name,
    )


def per_device(
    tiles,
    warmth_level,
    heat_flow_ability,
    material_zone_label,
    reciprocal_warming_storage,
    collector_potential_field,
    tab_indicator,
    sheet_node_link_matrix,
    solution_salt_level,
    grain_shell_level,
    solution_diffusion_matrix,
    grain_diffusion_matrix,
):
    sheets, _, span = warmth_level.shape
    shells, points, _, part = grain_shell_level.shape
    blocks = span // LANES
    nodes = points * part // LANES
    n = sheets * blocks
    edge = 2 * blocks
    size = 3 * n + edge

    def both_layers(pairs):
        return [(s * 2 + j, t * 2 + j) for s, t in pairs for j in range(2)]

    def across(where):
        return [(t * 2 + j, t * 2 + 1 - j) for t in where for j in range(2)]

    def mutual(pairs):
        return pairs + [(t, s) for s, t in pairs]

    def send(value, pairs):
        return lax.ppermute(value, ("tile", "layer"), pairs)

    cores = both_layers(mutual([(t, t + 1) for t in range(0, tiles, 2)]))
    beside = both_layers(mutual([(t, t - 1) for t in range(2, tiles, 2)]))
    beside = beside + across([0, tiles - 1])
    beyond = both_layers(mutual([(t, t - 3) for t in range(4, tiles, 2)]))
    beyond = beyond + across([0, 2, tiles - 3, tiles - 1])
    skipping = both_layers(mutual([(t, t + 3) for t in range(0, tiles - 3, 2)]))
    skipping = skipping + across([1, tiles - 2])
    layers = across(range(tiles))
    crossed = [(t * 2 + j, (t ^ 1) * 2 + 1 - j) for t in range(tiles) for j in range(2)]

    own = call(
        functools.partial(pack_kernel, blocks),
        "pack",
        shaped(3 * n + edge, LANES),
        [HBM] * 6,
        VMEM,
        1000,
        100000,
        (
            pltpu.SMEM(reciprocal_warming_storage.shape, jnp.float32),
            pltpu.VMEM((n, LANES), jnp.float32),
            pltpu.VMEM((n, LANES), jnp.int32),
            pltpu.VMEM((blocks, LANES), jnp.int32),
            pltpu.SemaphoreType.DMA((6,)),
        ),
    )(
        *in_hbm(
            reciprocal_warming_storage,
            warmth_level.reshape(n, LANES),
            heat_flow_ability.reshape(n, LANES),
            material_zone_label.reshape(n, LANES),
            collector_potential_field.reshape(n, LANES),
            tab_indicator.reshape(blocks, LANES),
        )
    )
    partner = send(own, cores)
    near = send(own, beside)
    skip = send(own, skipping)
    far = send(own[0 : 2 * n], beyond)
    held, local, factors = call(
        local_kernel,
        "columns",
        (
            shaped(shells, nodes, LANES),
            shaped(2 * nodes, LANES),
            shaped(shells, LANES),
        ),
        [HBM] * 4,
        (VMEM,) * 3,
        10**7,
        3000000,
        (
            pltpu.SMEM(grain_diffusion_matrix.shape, jnp.float32),
            pltpu.VMEM((nodes, LANES), jnp.float32),
            pltpu.VMEM(solution_diffusion_matrix.shape, jnp.float32),
            pltpu.SemaphoreType.DMA((3,)),
            pltpu.SemaphoreType.DMA((4,)),
        ),
    )(
        *in_hbm(
            grain_diffusion_matrix,
            grain_shell_level.reshape(shells, nodes, LANES),
            solution_salt_level.reshape(nodes, LANES),
            solution_diffusion_matrix,
        )
    )
    other_local = send(local, layers)
    near_in = send(near, cores)
    near, skip, far, held, local = lax.optimization_barrier((near, skip, far, held, local))
    skip_in = send(skip, cores)
    far_in = send(far, cores)
    mine, theirs, masks = call(
        functools.partial(sweep_kernel, sheets, blocks, tiles),
        "sweeps",
        (
            shaped(2 * n + 5 * edge, LANES),
            shaped(2 * n + 5 * edge, LANES),
            shaped(5 * edge, LANES),
        ),
        [VMEM] * 8,
        (VMEM,) * 3,
        10**6,
        500000,
    )(own, partner, near, skip, far, near_in, skip_in, far_in)
    other = send(theirs, crossed)
    masks, turned = lax.optimization_barrier((masks, sheet_node_link_matrix.T))
    link, turned = call(
        functools.partial(link_kernel, blocks, 2),
        "links",
        (shaped(points * blocks, 2 * n), shaped(n, points * blocks)),
        [VMEM],
        (VMEM, VMEM),
        10**6,
        100000,
    )(turned)
    held, masks, other_local = lax.optimization_barrier((held, masks, other_local))
    base = call(
        grain_kernel, "grains", shaped(shells, nodes, LANES), [VMEM] * 2, VMEM, 10**9, 3000000
    )(held, grain_diffusion_matrix)
    next_warmth, warming, flux, grain, salt = call(
        functools.partial(reaction_kernel, sheets, blocks),
        "reaction",
        (
            shaped(n, LANES),
            shaped(n, LANES),
            shaped(n, LANES),
            shaped(shells, nodes, LANES),
            shaped(nodes, LANES),
        ),
        [VMEM] * 9,
        (HBM,) * 5,
        10**7,
        3000000,
        (
            pltpu.VMEM((2 * n, 2 * LANES), jnp.float32),
            pltpu.VMEM((n, 2 * LANES), jnp.float32),
            pltpu.VMEM((shells, nodes, LANES), jnp.float32),
            pltpu.SemaphoreType.DMA((4,)),
            pltpu.SemaphoreType.DMA((4,)),
        ),
    )(factors, mine, other, local, other_local, masks, base, link, turned)
    return (
        next_warmth.reshape(warmth_level.shape),
        warming.reshape(warmth_level.shape),
        flux.reshape(warmth_level.shape),
        grain.reshape(grain_shell_level.shape),
        salt.reshape(solution_salt_level.shape),
    )


def solution(mesh):
    placed = (
        P("layer", "tile", None),
        P("layer", "tile", None),
        P("layer", "tile", None),
        P(),
        P("layer", "tile", None),
        P("tile", None),
        P(),
        P(None, "tile", "layer"),
        P(None, None, "tile", "layer"),
        P(),
        P(),
    )
    tiles, parts = mesh.shape["tile"], mesh.shape["layer"]
    plan = functools.partial(per_device, tiles) if parts == 2 else per_device_general
    return jax.shard_map(
        plan,
        mesh=mesh,
        in_specs=placed,
        out_specs=(
            P("layer", "tile", None),
            P("layer", "tile", None),
            P("layer", "tile", None),
            P(None, None, "tile", "layer"),
            P(None, "tile", "layer"),
        ),
        check_vma=False,
    )
```
